256 devices in a mesh: head: 8 (over y, z_lo), ctx: 32 (over z_hi, x, core).
Axes of the slice: x: 4, y: 4, z: 8 (z_hi: 4, z_lo: 2; z = z_hi * 2 + z_lo), core: 2. Of those that a mesh axis runs over, the one named last changes fastest.
Arguments:
- queries: bfloat16 [16384, 8192], P('ctx', 'head')
- key_states: bfloat16 [16384, 1024], P('ctx', 'head')
- values: bfloat16 [16384, 1024], P('ctx', 'head'), may hold values from -6 to 6
- out_weight: bfloat16 [8192, 8192], P('head', 'ctx'), may hold values from -0.125 to 0.125
- pair_table: int32 [3, 32], replicated, may hold values from 0 to 31, as said below
- block_order: int32 [128], replicated, may hold values from 0 to 127, each once
Outputs:
- projected: bfloat16 [16384, 8192], P('ctx', 'head')
The draws below stay inside these ranges and needn't reach their ends.
Inputs may be any that keep to these rules, and one draw needn't show every extreme that they name: `pair_table`: each of the 3 rows pairs rank i with rank i XOR m, with one mask m a row; the masks of the rows are distinct numbers from 1 to 31, and every bit of a rank is set in at least one of them. `block_order`: every block appears in exactly one slot.
All inputs are finite; a program needn't handle non-finite values.
Results may differ from the reference program's by a relative error of at most 0.017.
Values may be sent and summed in bfloat16 or wider, within the bound.
No kernel may reach another device: no remote copies, remote signals or barrier semaphores. Data moves between devices by JAX's collectives and lax.ppermute only.
A program may use at most 128 MiB of HBM per device.

```python
import jax
import jax.numpy as jnp
from jax import lax

D = 8192
HEADS = 64
KVH = 8
HD = 128
TOK_DEV = 512
BLOCK = 128
ROUNDS = 3
TOKENS = 16384
NBLK = 128
N_HEAD = 8
N_CTX = 32


def draw_queries(key, part):
    key = jax.random.fold_in(key, 11)
    result = jnp.clip(jax.random.normal(key, (TOKENS, HEADS * HD), jnp.float32), -4.5, 4.5)
    return result.astype(jnp.bfloat16)


def draw_key_states(key, part):
    key = jax.random.fold_in(key, 17)
    result = jnp.clip(jax.random.normal(key, (TOKENS, KVH * HD), jnp.float32), -4.5, 4.5)
    return result.astype(jnp.bfloat16)


def draw_pair_table(key, part):
    key = jax.random.fold_in(key, 23)
    bit_count = N_CTX.bit_length() - 1
    low_key, owner_key, extra_key = jax.random.split(key, 3)
    low_bits = jax.random.permutation(low_key, bit_count)[:ROUNDS].astype(jnp.int32)
    bit_ids = jnp.arange(bit_count, dtype=jnp.int32)
    round_ids = jnp.arange(ROUNDS, dtype=jnp.int32)
    bit_values = jnp.left_shift(jnp.ones((bit_count,), jnp.int32), bit_ids)
    is_low = jnp.any(bit_ids[None, :] == low_bits[:, None], axis=0)
    owner = jax.random.randint(owner_key, (bit_count,), 0, ROUNDS)
    extra = jax.random.randint(extra_key, (ROUNDS, bit_count), 0, 2)
    chosen = (owner[None, :] == round_ids[:, None]) | (extra == 1)
    chosen = chosen & jnp.logical_not(is_low)[None, :]
    chosen = chosen | (bit_ids[None, :] == low_bits[:, None])
    xor_masks = jnp.sum(jnp.where(chosen, bit_values[None, :], 0), axis=1).astype(jnp.int32)
    ranks = jnp.arange(N_CTX, dtype=jnp.int32)
    return jnp.bitwise_xor(ranks[None, :], xor_masks[:, None])


def with_spikes(entries, own_key, source, target, parts, factor):
    def block_of(dim):
        return (jnp.arange(entries.shape[dim]) // (entries.shape[dim] // parts)).reshape((-1,) + (1,) * (entries.ndim - 1 - dim))

    one_side = jax.random.permutation(own_key, parts)[block_of(target)]
    other_side = (block_of(target) + parts // 2) % parts
    return jnp.where((block_of(source) == one_side) | (block_of(source) == other_side), factor * entries, entries)


def level_of(own_key, extent, shards, smallest, high):
    gain = 1.0
    for dim, shards_of in shards:
        heights = jax.random.uniform(jax.random.fold_in(jax.random.fold_in(own_key, 6), dim), (shards_of,), jnp.float32, smallest / len(shards), high / len(shards))
        gain = gain * jnp.repeat(jnp.exp(heights), extent[dim] // shards_of).reshape((-1,) + (1,) * (len(extent) - 1 - dim))
    return gain


def centred(own_key, dims, scale, limit, pieces=(), kind=jnp.bfloat16):
    factor_of = level_of(own_key, dims, pieces, -0.22, 0.18) if pieces else 1.0
    values = jax.random.normal(own_key, dims, jnp.float32) * scale * factor_of
    return jnp.minimum(jnp.maximum(values, -limit), limit).astype(kind)


def heavy_noise(own_key, shape, spread, reach, cuts, heavy, kind=jnp.bfloat16):
    drawn = spread * jax.random.normal(own_key, shape, jnp.float32)
    if cuts:
        drawn = drawn * level_of(own_key, shape, cuts, -0.22, 0.18)
    return jnp.clip(with_spikes(drawn, jax.random.fold_in(own_key, 3), *heavy), -reach, reach).astype(kind)


def setup_inputs(seed: int = 0) -> dict:
    key_list = jax.random.split(jax.random.key(seed), 7)
    return {
        "queries": draw_queries(jax.random.fold_in(key_list[6], 71), 0),
        "key_states": draw_key_states(jax.random.fold_in(key_list[6], 71), 0),
        "values": centred(key_list[2], (TOKENS, KVH * HD), 1.0, 6.0, ((0, 32), (1, 8))),
        "out_weight": heavy_noise(key_list[3], (HEADS * HD, D), (HEADS * HD) ** -0.5, 0.125, ((0, 8), (1, 32)), (0, 1, 32, 2.75)),
        "pair_table": draw_pair_table(jax.random.fold_in(key_list[6], 71), 0),
        "block_order": jax.random.permutation(key_list[5], NBLK).astype(jnp.int32),
    }


def reference(queries, key_states, values, out_weight, pair_table, block_order):
    group = HEADS // KVH
    score_scale = HD ** -0.5
    offsets = jnp.arange(BLOCK, dtype=jnp.int32)
    positions = (block_order[:, None].astype(jnp.int32) * BLOCK + offsets[None, :]).reshape(-1)

    def one_rank(rank):
        ranks = jnp.concatenate([rank[None], pair_table[:, rank].astype(jnp.int32)])
        query_rows = lax.dynamic_slice_in_dim(queries, rank * TOK_DEV, TOK_DEV, 0)
        query_pos = lax.dynamic_slice_in_dim(positions, rank * TOK_DEV, TOK_DEV, 0)
        key_set = jnp.concatenate([lax.dynamic_slice_in_dim(key_states, ranks[i] * TOK_DEV, TOK_DEV, 0) for i in range(ROUNDS + 1)], axis=0)
        value_set = jnp.concatenate([lax.dynamic_slice_in_dim(values, ranks[i] * TOK_DEV, TOK_DEV, 0) for i in range(ROUNDS + 1)], axis=0)
        key_pos = jnp.concatenate([lax.dynamic_slice_in_dim(positions, ranks[i] * TOK_DEV, TOK_DEV, 0) for i in range(ROUNDS + 1)])
        allowed = key_pos[None, :] <= query_pos[:, None]

        def one_head(head):
            query_head = lax.dynamic_slice_in_dim(query_rows, head * HD, HD, 1)
            kv_col = (head // group) * HD
            key_head = lax.dynamic_slice_in_dim(key_set, kv_col, HD, 1)
            value_head = lax.dynamic_slice_in_dim(value_set, kv_col, HD, 1)
            scores = jnp.einsum("qd,kd->qk", query_head, key_head, preferred_element_type=jnp.float32) * score_scale
            scores = jnp.where(allowed, scores, -jnp.inf)
            row_max = jnp.max(scores, axis=1, keepdims=True)
            expo = jnp.exp(scores - row_max)
            weights = (expo / jnp.sum(expo, axis=1, keepdims=True)).astype(jnp.bfloat16)
            return jnp.dot(weights, value_head, preferred_element_type=jnp.float32).astype(jnp.bfloat16)

        per_head = lax.map(one_head, jnp.arange(HEADS, dtype=jnp.int32))
        return jnp.transpose(per_head, (1, 0, 2)).reshape(TOK_DEV, HEADS * HD)

    attn = lax.map(one_rank, jnp.arange(N_CTX, dtype=jnp.int32)).reshape(TOKENS, HEADS * HD)
    shard = HEADS * HD // N_HEAD
    total = jnp.zeros((TOKENS, D), jnp.float32)
    for group_index in range(N_HEAD):
        lower = group_index * shard
        partial_value = jnp.dot(attn[:, lower:lower + shard], out_weight[lower:lower + shard, :], preferred_element_type=jnp.float32).astype(jnp.bfloat16)
        total = total + partial_value.astype(jnp.float32)
    return total.astype(jnp.bfloat16)
```

```python
import math

import jax
import jax.numpy as jnp
from jax import lax
from jax.experimental import pallas as pl
from jax.experimental.pallas import tpu as pltpu
from jax.sharding import PartitionSpec as P

HD = 128
BLOCK = 128
ROUNDS = 3
SPAN = 4
GROUP = 2

CTX = [(z, x, c) for z in range(4) for x in range(4) for c in range(2)]
HEAD = [(y, s) for y in range(4) for s in range(2)]


def ctx_pairs(place):
    pairs = []
    for here in CTX:
        z, x, c = place(*here)
        pairs.append((here[0] * 8 + here[1] * 2 + here[2], z % 4 * 8 + x % 4 * 2 + c))
    return pairs


def head_pairs(place):
    pairs = []
    for here in HEAD:
        y, s = place(*here)
        pairs.append((here[0] * 2 + here[1], y % 4 * 2 + s))
    return pairs


def transpose_yz(arr):
    pairs = []
    for y, s in HEAD:
        for z, x, c in CTX:
            here = (y * 2 + s) * 32 + z * 8 + x * 2 + c
            pairs.append((here, (z * 2 + s) * 32 + y * 8 + x * 2 + c))
    return lax.ppermute(arr, ("head", "ctx"), pairs)


def to_y(arr, step):
    return lax.ppermute(arr, "head", head_pairs(lambda y, s: (y + step, s)))


def swap_low(arr):
    return lax.ppermute(arr, "head", head_pairs(lambda y, s: (y, 1 - s)))


def exchange(stacked, mask):
    ranks = len(CTX)

    def branch(m):
        return lambda arr: lax.ppermute(arr, "ctx", [(i, i ^ m) for i in range(ranks)])

    return lax.switch(mask - 1, [branch(m) for m in range(1, ranks)], stacked)


def attend_kernel(qid, kid, q_ref, kv0, others, out, kc, vc, qs, ms, ls, acc):
    srcs = [kv0] + [others.at[i] for i in range(ROUNDS)]
    hq = q_ref.shape[1] // HD
    blocks = q_ref.shape[0] // BLOCK
    factor = HD ** -0.5 * math.log2(math.e)
    width = SPAN * BLOCK
    tall = GROUP * BLOCK

    def one_block(i, carry):
        me = qid[i]
        rows = pl.ds(pl.multiple_of(i * BLOCK, BLOCK), BLOCK)
        kc[0:BLOCK, :] = kv0[0, rows, :]
        vc[0:BLOCK, :] = kv0[1, rows, :]
        n = jnp.int32(1)
        for j in range(blocks * (ROUNDS + 1)):
            take = kid[j] < me
            src = srcs[j // blocks]
            lo = j % blocks * BLOCK

            @pl.when(take)
            def _():
                dst = pl.ds(pl.multiple_of(n * BLOCK, BLOCK), BLOCK)
                kc[dst, :] = src[0, lo:lo + BLOCK, :]
                vc[dst, :] = src[1, lo:lo + BLOCK, :]

            n = n + take.astype(jnp.int32)
        for h in range(hq):
            qs[h * BLOCK:(h + 1) * BLOCK, :] = q_ref[rows, h * HD:(h + 1) * HD]

        def step(t, first):
            base = pl.multiple_of(t * width, width)
            kk = kc[pl.ds(base, width), :]
            vv = vc[pl.ds(base, width), :]
            col = lax.broadcasted_iota(jnp.int32, (tall, width), 1)
            if first:
                row = lax.broadcasted_iota(jnp.int32, (tall, width), 0) & (BLOCK - 1)
                ok = (col <= row) | ((col >= BLOCK) & (col < n * BLOCK))
            else:
                ok = col < n * BLOCK - base
            for g in range(hq // GROUP):
                r = slice(g * tall, (g + 1) * tall)
                s = lax.dot_general(qs[r, :], kk, (((1,), (1,)), ((), ())), preferred_element_type=jnp.float32)
                s = jnp.where(ok, s, -jnp.inf)
                top = jnp.max(s, axis=1, keepdims=True)
                if not first:
                    before = ms[r, 0:1]
                    top = jnp.maximum(before, top)
                    keep = jnp.exp2((before - top) * factor)
                p = jnp.exp2((s - top) * factor)
                total = jnp.sum(p, axis=1, keepdims=True)
                o = jnp.dot(p.astype(jnp.bfloat16), vv, preferred_element_type=jnp.float32)
                if not first:
                    total = keep * ls[r, 0:1] + total
                    o = keep * acc[r, :] + o
                ms[r, :] = jnp.broadcast_to(top, (tall, HD))
                ls[r, :] = jnp.broadcast_to(total, (tall, HD))
                acc[r, :] = o

        step(0, True)

        def body(t, c):
            step(t, False)
            return c

        lax.fori_loop(1, lax.div(n + (SPAN - 1), jnp.int32(SPAN)), body, 0)
        for h in range(hq):
            r = slice(h * BLOCK, (h + 1) * BLOCK)
            out[rows, h * HD:(h + 1) * HD] = (acc[r, :] / ls[r, :]).astype(jnp.bfloat16)
        return carry

    lax.fori_loop(0, blocks, one_block, 0)


def attend(query_ids, key_ids, queries, stacked, others):
    rows, cols = queries.shape
    tall = cols // HD * BLOCK
    room = rows * (ROUNDS + 1) + SPAN * BLOCK
    smem = pl.BlockSpec(memory_space=pltpu.SMEM)
    vmem = pl.BlockSpec(memory_space=pltpu.VMEM)
    return pl.pallas_call(
        attend_kernel,
        out_shape=jax.ShapeDtypeStruct(queries.shape, queries.dtype),
        in_specs=[smem, smem] + [vmem] * 3,
        out_specs=vmem,
        scratch_shapes=[pltpu.VMEM((room, HD), jnp.bfloat16)] * 2
        + [pltpu.VMEM((tall, HD), jnp.bfloat16)]
        + [pltpu.VMEM((tall, HD), jnp.float32)] * 3,
        compiler_params=pltpu.CompilerParams(vmem_limit_bytes=24 << 20),
        cost_estimate=pl.CostEstimate(flops=2 * rows * rows * 4 * cols * 2, bytes_accessed=4 << 20, transcendentals=rows * rows * 32),
    )(query_ids, key_ids, queries, stacked, others)


def project_kernel(info, a0, a1, a2, a3, w, out):
    total = None
    for step, a in enumerate((a0, a1, a2, a3)):
        term = jnp.dot(a[...], w[info[1 + step], 0], preferred_element_type=jnp.float32)
        total = term if total is None else total + term
    out[...] = total.astype(jnp.bfloat16)


def project(info, attn, weight, start, count):
    rows, depth = attn[0].shape
    cols = weight.shape[3]
    whole = pl.BlockSpec((rows, depth), lambda j, info: (0, 0))
    return pl.pallas_call(
        project_kernel,
        out_shape=jax.ShapeDtypeStruct((rows, count * cols), jnp.bfloat16),
        grid_spec=pltpu.PrefetchScalarGridSpec(
            num_scalar_prefetch=1,
            grid=(count,),
            in_specs=[whole] * 4 + [pl.BlockSpec((4, 1, depth, cols), lambda j, info: (0, info[start] + j, 0, 0))],
            out_specs=pl.BlockSpec((rows, cols), lambda j, info: (0, j)),
        ),
        compiler_params=pltpu.CompilerParams(vmem_limit_bytes=24 << 20),
        cost_estimate=pl.CostEstimate(flops=2 * rows * depth * 4 * cols * count, bytes_accessed=12 << 20, transcendentals=0),
    )(info, *attn, weight)


def add(*terms):
    total = terms[0].astype(jnp.float32)
    for term in terms[1:]:
        total = total + term.astype(jnp.float32)
    return total.astype(jnp.bfloat16)


def gather_y(attn):
    half = attn.shape[1] // 2
    below = to_y(attn, 1)
    above = to_y(attn, -1)
    left = to_y(below[:, :half], 1)
    right = to_y(above[:, half:], -1)
    return [attn, above, jnp.concatenate([left, right], axis=1), below]


def local(queries, key_states, values, out_weight, pair_table, block_order):
    rank = lax.axis_index("ctx")
    head = lax.axis_index("head")
    y, low = head // 2, head % 2

    weight = lax.all_gather(transpose_yz(out_weight), "ctx", axis=0)
    weight = weight.reshape((4, 8) + out_weight.shape)

    stacked = jnp.stack((key_states, values))
    masks = pair_table[:, 0]
    others = lax.map(lambda m: exchange(stacked, m), masks)

    blk_dev = queries.shape[0] // BLOCK

    def ids(r):
        return lax.dynamic_slice_in_dim(block_order, r * blk_dev, blk_dev, 0)

    query_ids = ids(rank)
    key_ids = jnp.concatenate([query_ids] + [ids(jnp.bitwise_xor(rank, masks[i])) for i in range(ROUNDS)])
    attn = gather_y(attend(query_ids, key_ids, queries, stacked, others))

    steps = jnp.arange(4, dtype=jnp.int32)
    sent, kept = 4 * (1 - low), 4 * low
    starts = jnp.stack([sent, sent + 2, kept, kept + 2])
    info = jnp.concatenate([jnp.zeros((1,), jnp.int32), (y + steps) % 4, starts]).astype(jnp.int32)
    arrived = [swap_low(project(info, attn, weight, 5 + i, 2)) for i in range(2)]
    ours = [project(info, attn, weight, 7 + i, 2) for i in range(2)]
    return jnp.concatenate([add(ours[i], arrived[i]) for i in range(2)], axis=1)


def solution(mesh):
    in_specs = (P("ctx", "head"), P("ctx", "head"), P("ctx", "head"), P("head", "ctx"), P(), P())
    return jax.shard_map(local, mesh=mesh, in_specs=in_specs, out_specs=P("ctx", "head"), check_vma=False)
```

```python
import math

import jax
import jax.numpy as jnp
from jax import lax
from jax.experimental import pallas as pl
from jax.experimental.pallas import tpu as pltpu
from jax.sharding import PartitionSpec as P

HD = 128
BLOCK = 128
ROUNDS = 3
SPAN = 4
GROUP = 2

CTX = [(z, x, c) for z in range(4) for x in range(4) for c in range(2)]
HEAD = [(y, s) for y in range(4) for s in range(2)]


def ctx_pairs(place):
    pairs = []
    for here in CTX:
        z, x, c = place(*here)
        pairs.append((here[0] * 8 + here[1] * 2 + here[2], z % 4 * 8 + x % 4 * 2 + c))
    return pairs


def head_pairs(place):
    pairs = []
    for here in HEAD:
        y, s = place(*here)
        pairs.append((here[0] * 2 + here[1], y % 4 * 2 + s))
    return pairs


def transpose_yz(arr):
    pairs = []
    for y, s in HEAD:
        for z, x, c in CTX:
            here = (y * 2 + s) * 32 + z * 8 + x * 2 + c
            pairs.append((here, (z * 2 + s) * 32 + y * 8 + x * 2 + c))
    return lax.ppermute(arr, ("head", "ctx"), pairs)


def to_y(arr, step):
    return lax.ppermute(arr, "head", head_pairs(lambda y, s: (y + step, s)))


def swap_low(arr):
    return lax.ppermute(arr, "head", head_pairs(lambda y, s: (y, 1 - s)))


def exchange(stacked, mask):
    ranks = len(CTX)

    def branch(m):
        return lambda arr: lax.ppermute(arr, "ctx", [(i, i ^ m) for i in range(ranks)])

    return lax.switch(mask - 1, [branch(m) for m in range(1, ranks)], stacked)


def attend_kernel(qid, kid, q_ref, kv0, others, out, kc, vc, qs, ms, ls, acc):
    srcs = [kv0] + [others.at[i] for i in range(ROUNDS)]
    hq = q_ref.shape[1] // HD
    blocks = q_ref.shape[0] // BLOCK
    factor = HD ** -0.5 * math.log2(math.e)
    width = SPAN * BLOCK
    tall = GROUP * BLOCK
    vc[...] = jnp.zeros_like(vc)

    def one_block(i, carry):
        me = qid[i]
        rows = pl.ds(pl.multiple_of(i * BLOCK, BLOCK), BLOCK)
        kc[0:BLOCK, :] = kv0[0, rows, :]
        vc[0:BLOCK, :] = kv0[1, rows, :]
        n = jnp.int32(1)
        for j in range(blocks * (ROUNDS + 1)):
            take = kid[j] < me
            src = srcs[j // blocks]
            lo = j % blocks * BLOCK

            @pl.when(take)
            def _():
                dst = pl.ds(pl.multiple_of(n * BLOCK, BLOCK), BLOCK)
                kc[dst, :] = src[0, lo:lo + BLOCK, :]
                vc[dst, :] = src[1, lo:lo + BLOCK, :]

            n = n + take.astype(jnp.int32)
        for h in range(hq):
            qs[h * BLOCK:(h + 1) * BLOCK, :] = q_ref[rows, h * HD:(h + 1) * HD]

        def step(t, first):
            base = pl.multiple_of(t * width, width)
            kk = kc[pl.ds(base, width), :]
            vv = vc[pl.ds(base, width), :]
            col = lax.broadcasted_iota(jnp.int32, (tall, width), 1)
            if first:
                row = lax.broadcasted_iota(jnp.int32, (tall, width), 0) & (BLOCK - 1)
                ok = (col <= row) | ((col >= BLOCK) & (col < n * BLOCK))
            else:
                ok = col < n * BLOCK - base
            for g in range(hq // GROUP):
                r = slice(g * tall, (g + 1) * tall)
                s = lax.dot_general(qs[r, :], kk, (((1,), (1,)), ((), ())), preferred_element_type=jnp.float32)
                s = jnp.where(ok, s, -jnp.inf)
                top = jnp.max(s, axis=1, keepdims=True)
                if not first:
                    before = ms[r, 0:1]
                    top = jnp.maximum(before, top)
                    keep = jnp.exp2((before - top) * factor)
                p = jnp.exp2((s - top) * factor)
                total = jnp.sum(p, axis=1, keepdims=True)
                o = jnp.dot(p.astype(jnp.bfloat16), vv, preferred_element_type=jnp.float32)
                if not first:
                    total = keep * ls[r, 0:1] + total
                    o = keep * acc[r, :] + o
                ms[r, :] = jnp.broadcast_to(top, (tall, HD))
                ls[r, :] = jnp.broadcast_to(total, (tall, HD))
                acc[r, :] = o

        step(0, True)

        def body(t, c):
            step(t, False)
            return c

        lax.fori_loop(1, lax.div(n + (SPAN - 1), jnp.int32(SPAN)), body, 0)
        for h in range(hq):
            r = slice(h * BLOCK, (h + 1) * BLOCK)
            out[rows, h * HD:(h + 1) * HD] = (acc[r, :] / ls[r, :]).astype(jnp.bfloat16)
        return carry

    lax.fori_loop(0, blocks, one_block, 0)


def attend(query_ids, key_ids, queries, stacked, others):
    rows, cols = queries.shape
    tall = cols // HD * BLOCK
    room = rows * (ROUNDS + 1) + SPAN * BLOCK
    smem = pl.BlockSpec(memory_space=pltpu.SMEM)
    vmem = pl.BlockSpec(memory_space=pltpu.VMEM)
    return pl.pallas_call(
        attend_kernel,
        out_shape=jax.ShapeDtypeStruct(queries.shape, queries.dtype),
        in_specs=[smem, smem] + [vmem] * 3,
        out_specs=vmem,
        scratch_shapes=[pltpu.VMEM((room, HD), jnp.bfloat16)] * 2
        + [pltpu.VMEM((tall, HD), jnp.bfloat16)]
        + [pltpu.VMEM((tall, HD), jnp.float32)] * 3,
        compiler_params=pltpu.CompilerParams(vmem_limit_bytes=24 << 20),
        cost_estimate=pl.CostEstimate(flops=2 * rows * rows * 4 * cols * 2, bytes_accessed=4 << 20, transcendentals=rows * rows * 32),
    )(query_ids, key_ids, queries, stacked, others)


def project_kernel(info, a0, a1, a2, a3, w, out):
    total = None
    for step, a in enumerate((a0, a1, a2, a3)):
        term = jnp.dot(a[...], w[info[1 + step], 0], preferred_element_type=jnp.float32)
        total = term if total is None else total + term
    out[...] = total.astype(jnp.bfloat16)


def project(info, attn, weight, start, count):
    rows, depth = attn[0].shape
    cols = weight.shape[3]
    whole = pl.BlockSpec((rows, depth), lambda j, info: (0, 0))
    return pl.pallas_call(
        project_kernel,
        out_shape=jax.ShapeDtypeStruct((rows, count * cols), jnp.bfloat16),
        grid_spec=pltpu.PrefetchScalarGridSpec(
            num_scalar_prefetch=1,
            grid=(count,),
            in_specs=[whole] * 4 + [pl.BlockSpec((4, 1, depth, cols), lambda j, info: (0, info[start] + j, 0, 0))],
            out_specs=pl.BlockSpec((rows, cols), lambda j, info: (0, j)),
        ),
        compiler_params=pltpu.CompilerParams(vmem_limit_bytes=52 << 20),
        cost_estimate=pl.CostEstimate(flops=2 * rows * depth * 4 * cols * count, bytes_accessed=12 << 20, transcendentals=0),
    )(info, *attn, weight)


def add(*terms):
    total = terms[0].astype(jnp.float32)
    for term in terms[1:]:
        total = total + term.astype(jnp.float32)
    return total.astype(jnp.bfloat16)


def gather_y(attn):
    half = attn.shape[1] // 2
    below = to_y(attn, 1)
    above = to_y(attn, -1)
    left = to_y(below[:, :half], 1)
    right = to_y(above[:, half:], -1)
    return [attn, above, jnp.concatenate([left, right], axis=1), below]


def local(queries, key_states, values, out_weight, pair_table, block_order):
    rank = lax.axis_index("ctx")
    head = lax.axis_index("head")
    y, low = head // 2, head % 2

    moved = transpose_yz(out_weight)
    stacked = jnp.stack((key_states, values))
    masks = pair_table[:, 0]
    others = lax.map(lambda m: exchange(stacked, m), masks)
    moved, others = lax.optimization_barrier((moved, others))
    weight = lax.all_gather(moved, "ctx", axis=0)
    weight = weight.reshape((4, 8) + out_weight.shape)

    blk_dev = queries.shape[0] // BLOCK

    def ids(r):
        return lax.dynamic_slice_in_dim(block_order, r * blk_dev, blk_dev, 0)

    query_ids = ids(rank)
    key_ids = jnp.concatenate([query_ids] + [ids(jnp.bitwise_xor(rank, masks[i])) for i in range(ROUNDS)])
    attn = gather_y(attend(query_ids, key_ids, queries, stacked, others))

    steps = jnp.arange(4, dtype=jnp.int32)
    sent, kept = 4 * (1 - low), 4 * low
    starts = jnp.stack([sent, sent + 2, kept])
    info = jnp.concatenate([jnp.zeros((1,), jnp.int32), (y + steps) % 4, starts]).astype(jnp.int32)
    arrived = [swap_low(project(info, attn, weight, 5 + i, 2)) for i in range(2)]
    ours = project(info, attn, weight, 7, 4)
    return add(ours, jnp.concatenate(arrived, axis=1))


def solution(mesh):
    in_specs = (P("ctx", "head"), P("ctx", "head"), P("ctx", "head"), P("head", "ctx"), P(), P())
    return jax.shard_map(local, mesh=mesh, in_specs=in_specs, out_specs=P("ctx", "head"), check_vma=False)
```

```python
import math

import jax
import jax.numpy as jnp
from jax import lax
from jax.experimental import pallas as pl
from jax.experimental.pallas import tpu as pltpu
from jax.sharding import PartitionSpec as P

HD = 128
BLOCK = 128
ROUNDS = 3
SPAN = 4
GROUP = 2

CTX = [(z, x, c) for z in range(4) for x in range(4) for c in range(2)]
HEAD = [(y, s) for y in range(4) for s in range(2)]


def ctx_pairs(place):
    pairs = []
    for here in CTX:
        z, x, c = place(*here)
        pairs.append((here[0] * 8 + here[1] * 2 + here[2], z % 4 * 8 + x % 4 * 2 + c))
    return pairs


def head_pairs(place):
    pairs = []
    for here in HEAD:
        y, s = place(*here)
        pairs.append((here[0] * 2 + here[1], y % 4 * 2 + s))
    return pairs


def to_columns(arr):
    pairs = []
    for y, s in HEAD:
        for z, x, c in CTX:
            here = (y * 2 + s) * 32 + z * 8 + x * 2 + c
            pairs.append((here, (z * 2 + x // 2) * 32 + y * 8 + (s * 2 + x % 2) * 2 + c))
    return lax.ppermute(arr, ("head", "ctx"), pairs)


def to_y(arr, step):
    return lax.ppermute(arr, "head", head_pairs(lambda y, s: (y + step, s)))


def swap_low(arr):
    return lax.ppermute(arr, "head", head_pairs(lambda y, s: (y, 1 - s)))


def exchange(stacked, mask):
    ranks = len(CTX)

    def branch(m):
        return lambda arr: lax.ppermute(arr, "ctx", [(i, i ^ m) for i in range(ranks)])

    return lax.switch(mask - 1, [branch(m) for m in range(1, ranks)], stacked)


def attend_kernel(qid, kid, q_ref, kv0, others, out, kc, vc, qs, ms, ls, acc):
    srcs = [kv0] + [others.at[i] for i in range(ROUNDS)]
    hq = q_ref.shape[1] // HD
    blocks = q_ref.shape[0] // BLOCK
    factor = HD ** -0.5 * math.log2(math.e)
    width = SPAN * BLOCK
    tall = GROUP * BLOCK
    vc[...] = jnp.zeros_like(vc)

    def one_block(i, carry):
        me = qid[i]
        rows = pl.ds(pl.multiple_of(i * BLOCK, BLOCK), BLOCK)
        kc[0:BLOCK, :] = kv0[0, rows, :]
        vc[0:BLOCK, :] = kv0[1, rows, :]
        n = jnp.int32(1)
        for j in range(blocks * (ROUNDS + 1)):
            take = kid[j] < me
            src = srcs[j // blocks]
            lo = j % blocks * BLOCK

            @pl.when(take)
            def _():
                dst = pl.ds(pl.multiple_of(n * BLOCK, BLOCK), BLOCK)
                kc[dst, :] = src[0, lo:lo + BLOCK, :]
                vc[dst, :] = src[1, lo:lo + BLOCK, :]

            n = n + take.astype(jnp.int32)
        for h in range(hq):
            qs[h * BLOCK:(h + 1) * BLOCK, :] = q_ref[rows, h * HD:(h + 1) * HD]

        def step(t, first):
            base = pl.multiple_of(t * width, width)
            kk = kc[pl.ds(base, width), :]
            vv = vc[pl.ds(base, width), :]
            col = lax.broadcasted_iota(jnp.int32, (tall, width), 1)
            if first:
                row = lax.broadcasted_iota(jnp.int32, (tall, width), 0) & (BLOCK - 1)
                ok = (col <= row) | ((col >= BLOCK) & (col < n * BLOCK))
            else:
                ok = col < n * BLOCK - base
            for g in range(hq // GROUP):
                r = slice(g * tall, (g + 1) * tall)
                s = lax.dot_general(qs[r, :], kk, (((1,), (1,)), ((), ())), preferred_element_type=jnp.float32)
                s = jnp.where(ok, s, -jnp.inf)
                top = jnp.max(s, axis=1, keepdims=True)
                if not first:
                    before = ms[r, 0:1]
                    top = jnp.maximum(before, top)
                    keep = jnp.exp2((before - top) * factor)
                p = jnp.exp2((s - top) * factor)
                total = jnp.sum(p, axis=1, keepdims=True)
                o = jnp.dot(p.astype(jnp.bfloat16), vv, preferred_element_type=jnp.float32)
                if not first:
                    total = keep * ls[r, 0:1] + total
                    o = keep * acc[r, :] + o
                ms[r, :] = jnp.broadcast_to(top, (tall, HD))
                ls[r, :] = jnp.broadcast_to(total, (tall, HD))
                acc[r, :] = o

        step(0, True)

        def body(t, c):
            step(t, False)
            return c

        lax.fori_loop(1, lax.div(n + (SPAN - 1), jnp.int32(SPAN)), body, 0)
        for h in range(hq):
            r = slice(h * BLOCK, (h + 1) * BLOCK)
            out[rows, h * HD:(h + 1) * HD] = (acc[r, :] / ls[r, :]).astype(jnp.bfloat16)
        return carry

    lax.fori_loop(0, blocks, one_block, 0)


def attend(query_ids, key_ids, queries, stacked, others):
    rows, cols = queries.shape
    tall = cols // HD * BLOCK
    room = rows * (ROUNDS + 1) + SPAN * BLOCK
    smem = pl.BlockSpec(memory_space=pltpu.SMEM)
    vmem = pl.BlockSpec(memory_space=pltpu.VMEM)
    return pl.pallas_call(
        attend_kernel,
        out_shape=jax.ShapeDtypeStruct(queries.shape, queries.dtype),
        in_specs=[smem, smem] + [vmem] * 3,
        out_specs=vmem,
        scratch_shapes=[pltpu.VMEM((room, HD), jnp.bfloat16)] * 2
        + [pltpu.VMEM((tall, HD), jnp.bfloat16)]
        + [pltpu.VMEM((tall, HD), jnp.float32)] * 3,
        compiler_params=pltpu.CompilerParams(vmem_limit_bytes=24 << 20),
        cost_estimate=pl.CostEstimate(flops=2 * rows * rows * 4 * cols * 2, bytes_accessed=4 << 20, transcendentals=rows * rows * 32),
    )(query_ids, key_ids, queries, stacked, others)


def project_kernel(info, a0, a1, a2, a3, w, out):
    depth = w.shape[2]
    total = None
    for step, a in enumerate((a0, a1, a2, a3)):
        for side in range(2):
            block = w[info[2 * step + side], 0]
            term = jnp.dot(a[:, side * depth:(side + 1) * depth], block, preferred_element_type=jnp.float32)
            total = term if total is None else total + term
    out[...] = total.astype(jnp.bfloat16)


def project(info, attn, weight):
    groups, tiles, depth, cols = weight.shape
    rows = attn[0].shape[0]
    return pl.pallas_call(
        project_kernel,
        out_shape=jax.ShapeDtypeStruct((rows, tiles * cols), jnp.bfloat16),
        grid_spec=pltpu.PrefetchScalarGridSpec(
            num_scalar_prefetch=1,
            grid=(tiles,),
            in_specs=[pl.BlockSpec(memory_space=pltpu.VMEM)] * 4
            + [pl.BlockSpec((groups, 1, depth, cols), lambda j, info: (0, j, 0, 0))],
            out_specs=pl.BlockSpec((rows, cols), lambda j, info: (0, j)),
        ),
        compiler_params=pltpu.CompilerParams(vmem_limit_bytes=46 << 20),
        cost_estimate=pl.CostEstimate(flops=2 * rows * depth * groups * cols * tiles, bytes_accessed=25 << 20, transcendentals=0),
    )(info, *attn, weight)


def gather_y(attn):
    half = attn.shape[1] // 2
    below = to_y(attn, 1)
    above = to_y(attn, -1)
    left = to_y(below[:, :half], 1)
    right = to_y(above[:, half:], -1)
    return [attn, above, jnp.concatenate([left, right], axis=1), below]


def local(queries, key_states, values, out_weight, pair_table, block_order):
    rank = lax.axis_index("ctx")
    head = lax.axis_index("head")
    y, low = head // 2, head % 2

    stacked = jnp.stack((key_states, values))
    masks = pair_table[:, 0]
    others = lax.map(lambda m: exchange(stacked, m), masks)
    out_weight, others = lax.optimization_barrier((out_weight, others))
    moved = to_columns(out_weight)

    blk_dev = queries.shape[0] // BLOCK

    def ids(r):
        return lax.dynamic_slice_in_dim(block_order, r * blk_dev, blk_dev, 0)

    query_ids = ids(rank)
    key_ids = jnp.concatenate([query_ids] + [ids(jnp.bitwise_xor(rank, masks[i])) for i in range(ROUNDS)])
    attn = attend(query_ids, key_ids, queries, stacked, others)
    moved, attn = lax.optimization_barrier((moved, attn))
    weight = lax.all_gather(moved, "ctx", axis=0)
    weight = weight.reshape((8, 4) + out_weight.shape)
    attn = gather_y(jnp.concatenate([attn, swap_low(attn)], axis=1))

    info = jnp.stack([(y + step) % 4 * 2 + side for step in range(4) for side in (low, 1 - low)])
    return project(info.astype(jnp.int32), attn, weight)


def solution(mesh):
    in_specs = (P("ctx", "head"), P("ctx", "head"), P("ctx", "head"), P("head", "ctx"), P(), P())
    return jax.shard_map(local, mesh=mesh, in_specs=in_specs, out_specs=P("ctx", "head"), check_vma=False)
```

```python
import math

import jax
import jax.numpy as jnp
from jax import lax
from jax.experimental import pallas as pl
from jax.experimental.pallas import tpu as pltpu
from jax.sharding import PartitionSpec as P

HD = 128
BLOCK = 128
ROUNDS = 3
SPAN = 4
GROUP = 2

CTX = [(z, x, c) for z in range(4) for x in range(4) for c in range(2)]
HEAD = [(y, s) for y in range(4) for s in range(2)]


def ctx_pairs(place):
    pairs = []
    for here in CTX:
        z, x, c = place(*here)
        pairs.append((here[0] * 8 + here[1] * 2 + here[2], z % 4 * 8 + x % 4 * 2 + c))
    return pairs


def head_pairs(place):
    pairs = []
    for here in HEAD:
        y, s = place(*here)
        pairs.append((here[0] * 2 + here[1], y % 4 * 2 + s))
    return pairs


def transpose_yz(arr):
    pairs = []
    for y, s in HEAD:
        for z, x, c in CTX:
            here = (y * 2 + s) * 32 + z * 8 + x * 2 + c
            pairs.append((here, (z * 2 + s) * 32 + y * 8 + x * 2 + c))
    return lax.ppermute(arr, ("head", "ctx"), pairs)


def from_sibling(arr):
    return lax.ppermute(arr, "ctx", ctx_pairs(lambda z, x, c: (z, x, 1 - c)))


def to_y(arr, step):
    return lax.ppermute(arr, "head", head_pairs(lambda y, s: (y + step, s)))


def swap_low(arr):
    return lax.ppermute(arr, "head", head_pairs(lambda y, s: (y, 1 - s)))


def exchange(stacked, mask):
    ranks = len(CTX)

    def branch(m):
        return lambda arr: lax.ppermute(arr, "ctx", [(i, i ^ m) for i in range(ranks)])

    return lax.switch(mask - 1, [branch(m) for m in range(1, ranks)], stacked)


def attend_kernel(qid, kid, q_ref, kv0, others, out, kc, vc, qs, ms, ls, acc):
    srcs = [kv0] + [others.at[i] for i in range(ROUNDS)]
    hq = q_ref.shape[1] // HD
    blocks = q_ref.shape[0] // BLOCK
    factor = HD ** -0.5 * math.log2(math.e)
    width = SPAN * BLOCK
    tall = GROUP * BLOCK
    vc[...] = jnp.zeros_like(vc)

    def one_block(i, carry):
        me = qid[i]
        rows = pl.ds(pl.multiple_of(i * BLOCK, BLOCK), BLOCK)
        kc[0:BLOCK, :] = kv0[0, rows, :]
        vc[0:BLOCK, :] = kv0[1, rows, :]
        n = jnp.int32(1)
        for j in range(blocks * (ROUNDS + 1)):
            take = kid[j] < me
            src = srcs[j // blocks]
            lo = j % blocks * BLOCK

            @pl.when(take)
            def _():
                dst = pl.ds(pl.multiple_of(n * BLOCK, BLOCK), BLOCK)
                kc[dst, :] = src[0, lo:lo + BLOCK, :]
                vc[dst, :] = src[1, lo:lo + BLOCK, :]

            n = n + take.astype(jnp.int32)
        for h in range(hq):
            qs[h * BLOCK:(h + 1) * BLOCK, :] = q_ref[rows, h * HD:(h + 1) * HD]

        def step(t, first):
            base = pl.multiple_of(t * width, width)
            kk = kc[pl.ds(base, width), :]
            vv = vc[pl.ds(base, width), :]
            col = lax.broadcasted_iota(jnp.int32, (tall, width), 1)
            if first:
                row = lax.broadcasted_iota(jnp.int32, (tall, width), 0) & (BLOCK - 1)
                ok = (col <= row) | ((col >= BLOCK) & (col < n * BLOCK))
            else:
                ok = col < n * BLOCK - base
            for g in range(hq // GROUP):
                r = slice(g * tall, (g + 1) * tall)
                s = lax.dot_general(qs[r, :], kk, (((1,), (1,)), ((), ())), preferred_element_type=jnp.float32)
                s = jnp.where(ok, s, -jnp.inf)
                top = jnp.max(s, axis=1, keepdims=True)
                if not first:
                    before = ms[r, 0:1]
                    top = jnp.maximum(before, top)
                    keep = jnp.exp2((before - top) * factor)
                p = jnp.exp2((s - top) * factor)
                total = jnp.sum(p, axis=1, keepdims=True)
                o = jnp.dot(p.astype(jnp.bfloat16), vv, preferred_element_type=jnp.float32)
                if not first:
                    total = keep * ls[r, 0:1] + total
                    o = keep * acc[r, :] + o
                ms[r, :] = jnp.broadcast_to(top, (tall, HD))
                ls[r, :] = jnp.broadcast_to(total, (tall, HD))
                acc[r, :] = o

        step(0, True)

        def body(t, c):
            step(t, False)
            return c

        lax.fori_loop(1, lax.div(n + (SPAN - 1), jnp.int32(SPAN)), body, 0)
        for h in range(hq):
            r = slice(h * BLOCK, (h + 1) * BLOCK)
            out[rows, h * HD:(h + 1) * HD] = (acc[r, :] / ls[r, :]).astype(jnp.bfloat16)
        return carry

    lax.fori_loop(0, blocks, one_block, 0)


def attend(query_ids, key_ids, queries, stacked, others):
    rows, cols = queries.shape
    tall = cols // HD * BLOCK
    room = rows * (ROUNDS + 1) + SPAN * BLOCK
    smem = pl.BlockSpec(memory_space=pltpu.SMEM)
    vmem = pl.BlockSpec(memory_space=pltpu.VMEM)
    return pl.pallas_call(
        attend_kernel,
        out_shape=jax.ShapeDtypeStruct(queries.shape, queries.dtype),
        in_specs=[smem, smem] + [vmem] * 3,
        out_specs=vmem,
        scratch_shapes=[pltpu.VMEM((room, HD), jnp.bfloat16)] * 2
        + [pltpu.VMEM((tall, HD), jnp.bfloat16)]
        + [pltpu.VMEM((tall, HD), jnp.float32)] * 3,
        compiler_params=pltpu.CompilerParams(vmem_limit_bytes=24 << 20),
        cost_estimate=pl.CostEstimate(flops=2 * rows * rows * 4 * cols * 2, bytes_accessed=4 << 20, transcendentals=rows * rows * 32),
    )(query_ids, key_ids, queries, stacked, others)


def project_kernel(info, a0, a1, a2, a3, w, out):
    total = None
    for step, a in enumerate((a0, a1, a2, a3)):
        term = jnp.dot(a[...], w[info[1 + step], 0], preferred_element_type=jnp.float32)
        total = term if total is None else total + term
    out[...] = total.astype(jnp.bfloat16)


def project(info, attn, weight, start, count):
    rows, depth = attn[0].shape
    cols = weight.shape[3]
    whole = pl.BlockSpec((rows, depth), lambda j, info: (0, 0))
    return pl.pallas_call(
        project_kernel,
        out_shape=jax.ShapeDtypeStruct((rows, count * cols), jnp.bfloat16),
        grid_spec=pltpu.PrefetchScalarGridSpec(
            num_scalar_prefetch=1,
            grid=(count,),
            in_specs=[whole] * 4 + [pl.BlockSpec((4, 1, depth, cols), lambda j, info: (0, info[start] + j, 0, 0))],
            out_specs=pl.BlockSpec((rows, cols), lambda j, info: (0, j)),
        ),
        compiler_params=pltpu.CompilerParams(vmem_limit_bytes=52 << 20),
        cost_estimate=pl.CostEstimate(flops=2 * rows * depth * 4 * cols * count, bytes_accessed=12 << 20, transcendentals=0),
    )(info, *attn, weight)


def first_kernel(info, attn, w, up, down):
    a = attn[...]
    cols = w.shape[3]
    for x in range(4):
        out = (up, down)[x // 2]
        at = x % 2 * cols
        out[:, at:at + cols] = jnp.dot(a, w[info[2], x], preferred_element_type=jnp.float32).astype(jnp.bfloat16)


def rest_kernel(info, attn, w, up, down, own):
    a = attn[...]
    cols = w.shape[3]
    for step, out in ((1, up), (3, down), (0, own)):
        for x in range(4):
            at = x * cols
            out[:, at:at + cols] = jnp.dot(a, w[info[step], x], preferred_element_type=jnp.float32).astype(jnp.bfloat16)


def pieces(kernel, info, attn, weight, widths):
    rows, depth = attn.shape
    smem = pl.BlockSpec(memory_space=pltpu.SMEM)
    vmem = pl.BlockSpec(memory_space=pltpu.VMEM)
    return pl.pallas_call(
        kernel,
        out_shape=[jax.ShapeDtypeStruct((rows, width), jnp.bfloat16) for width in widths],
        in_specs=[smem, vmem, vmem],
        out_specs=[vmem] * len(widths),
        compiler_params=pltpu.CompilerParams(vmem_limit_bytes=24 << 20),
        cost_estimate=pl.CostEstimate(flops=2 * rows * depth * sum(widths), bytes_accessed=10 << 20, transcendentals=0),
    )(info, attn, weight)


def reduce_y(info, attn, weight):
    cols = 2 * weight.shape[3]
    up2, down2 = pieces(first_kernel, info, attn, weight, (cols, cols))
    a, b = to_y(up2, 1), to_y(down2, -1)
    up, down, own = pieces(rest_kernel, info, attn, weight, (2 * cols,) * 3)
    up = jnp.concatenate([add(up[:, :cols], a), up[:, cols:]], axis=1)
    down = jnp.concatenate([down[:, :cols], add(down[:, cols:], b)], axis=1)
    return own, to_y(up, 1), to_y(down, -1)


def add(*terms):
    total = terms[0].astype(jnp.float32)
    for term in terms[1:]:
        total = total + term.astype(jnp.float32)
    return total.astype(jnp.bfloat16)


def gather_y(attn):
    half = attn.shape[1] // 2
    below = to_y(attn, 1)
    above = to_y(attn, -1)
    left = to_y(below[:, :half], 1)
    right = to_y(above[:, half:], -1)
    return [attn, above, jnp.concatenate([left, right], axis=1), below]


def local(queries, key_states, values, out_weight, pair_table, block_order):
    rank = lax.axis_index("ctx")
    head = lax.axis_index("head")
    y, low = head // 2, head % 2
    core = rank % 2
    depth, cols = out_weight.shape

    upper, lower = out_weight[:depth // 2], out_weight[depth // 2:]
    mine = jnp.where(core == 0, upper, lower)
    swapped = from_sibling(jnp.where(core == 0, lower, upper))
    first = lax.all_gather(jnp.where(core == 0, mine, swapped), "ctx", axis=0)
    first = first.reshape((4, 4, depth, cols))
    moved = transpose_yz(jnp.where(core == 0, swapped, mine))

    stacked = jnp.stack((key_states, values))
    masks = pair_table[:, 0]
    others = lax.map(lambda m: exchange(stacked, m), masks)
    moved, others = lax.optimization_barrier((moved, others))
    second = lax.all_gather(moved, "ctx", axis=0)
    second = second.reshape((4, 4, depth, cols))

    blk_dev = queries.shape[0] // BLOCK

    def ids(r):
        return lax.dynamic_slice_in_dim(block_order, r * blk_dev, blk_dev, 0)

    query_ids = ids(rank)
    key_ids = jnp.concatenate([query_ids] + [ids(jnp.bitwise_xor(rank, masks[i])) for i in range(ROUNDS)])
    attn = attend(query_ids, key_ids, queries, stacked, others)
    gathered = gather_y(attn)

    groups = ((y + jnp.arange(4, dtype=jnp.int32)) % 4).astype(jnp.int32)
    gathered, attn, groups = lax.optimization_barrier((gathered, attn, groups))
    terms = reduce_y(groups, attn, first)
    half = 2 * cols

    def side(arr, s):
        return jnp.where(s == 0, arr[:, :half], arr[:, half:])

    sent = add(*[side(t, 1 - low) for t in terms])
    sent, gathered = lax.optimization_barrier((sent, gathered))
    core0 = add(*[side(t, low) for t in terms], swap_low(sent))

    info = jnp.concatenate([jnp.zeros((1,), jnp.int32), groups, jnp.stack([2 * (1 - low), 2 * low]).astype(jnp.int32)])
    arrived = swap_low(project(info, gathered, second, 5, 2))
    core1 = add(project(info, gathered, second, 6, 2), arrived)
    return jnp.concatenate([core0[:, :cols], core1[:, :cols], core0[:, cols:], core1[:, cols:]], axis=1)


def solution(mesh):
    in_specs = (P("ctx", "head"), P("ctx", "head"), P("ctx", "head"), P("head", "ctx"), P(), P())
    return jax.shard_map(local, mesh=mesh, in_specs=in_specs, out_specs=P("ctx", "head"), check_vma=False)
```

```python
import math

import jax
import jax.numpy as jnp
from jax import lax
from jax.experimental import pallas as pl
from jax.experimental.pallas import tpu as pltpu
from jax.sharding import PartitionSpec as P

HD = 128
BLOCK = 128
ROUNDS = 3
SPAN = 4
GROUP = 2

CTX = [(z, x, c) for z in range(4) for x in range(4) for c in range(2)]
HEAD = [(y, s) for y in range(4) for s in range(2)]


def ctx_pairs(place):
    pairs = []
    for here in CTX:
        z, x, c = place(*here)
        pairs.append((here[0] * 8 + here[1] * 2 + here[2], z % 4 * 8 + x % 4 * 2 + c))
    return pairs


def head_pairs(place):
    pairs = []
    for here in HEAD:
        y, s = place(*here)
        pairs.append((here[0] * 2 + here[1], y % 4 * 2 + s))
    return pairs


def transpose_yz(arr):
    pairs = []
    for y, s in HEAD:
        for z, x, c in CTX:
            here = (y * 2 + s) * 32 + z * 8 + x * 2 + c
            pairs.append((here, (z * 2 + s) * 32 + y * 8 + x * 2 + c))
    return lax.ppermute(arr, ("head", "ctx"), pairs)


def from_sibling(arr):
    return lax.ppermute(arr, "ctx", ctx_pairs(lambda z, x, c: (z, x, 1 - c)))


def to_y(arr, step):
    return lax.ppermute(arr, "head", head_pairs(lambda y, s: (y + step, s)))


def swap_low(arr):
    return lax.ppermute(arr, "head", head_pairs(lambda y, s: (y, 1 - s)))


def exchange(stacked, mask):
    ranks = len(CTX)

    def branch(m):
        return lambda arr: lax.ppermute(arr, "ctx", [(i, i ^ m) for i in range(ranks)])

    return lax.switch(mask - 1, [branch(m) for m in range(1, ranks)], stacked)


def attend_kernel(qid, kid, q_ref, kv0, others, out, kc, vc, qs, ms, ls, acc):
    srcs = [kv0] + [others.at[i] for i in range(ROUNDS)]
    hq = q_ref.shape[1] // HD
    blocks = q_ref.shape[0] // BLOCK
    factor = HD ** -0.5 * math.log2(math.e)
    width = SPAN * BLOCK
    tall = GROUP * BLOCK
    vc[...] = jnp.zeros_like(vc)

    def one_block(i, carry):
        me = qid[i]
        rows = pl.ds(pl.multiple_of(i * BLOCK, BLOCK), BLOCK)
        kc[0:BLOCK, :] = kv0[0, rows, :]
        vc[0:BLOCK, :] = kv0[1, rows, :]
        n = jnp.int32(1)
        for j in range(blocks * (ROUNDS + 1)):
            take = kid[j] < me
            src = srcs[j // blocks]
            lo = j % blocks * BLOCK

            @pl.when(take)
            def _():
                dst = pl.ds(pl.multiple_of(n * BLOCK, BLOCK), BLOCK)
                kc[dst, :] = src[0, lo:lo + BLOCK, :]
                vc[dst, :] = src[1, lo:lo + BLOCK, :]

            n = n + take.astype(jnp.int32)
        for h in range(hq):
            qs[h * BLOCK:(h + 1) * BLOCK, :] = q_ref[rows, h * HD:(h + 1) * HD]

        def step(t, first):
            base = pl.multiple_of(t * width, width)
            kk = kc[pl.ds(base, width), :]
            vv = vc[pl.ds(base, width), :]
            col = lax.broadcasted_iota(jnp.int32, (tall, width), 1)
            if first:
                row = lax.broadcasted_iota(jnp.int32, (tall, width), 0) & (BLOCK - 1)
                ok = (col <= row) | ((col >= BLOCK) & (col < n * BLOCK))
            else:
                ok = col < n * BLOCK - base
            for g in range(hq // GROUP):
                r = slice(g * tall, (g + 1) * tall)
                s = lax.dot_general(qs[r, :], kk, (((1,), (1,)), ((), ())), preferred_element_type=jnp.float32)
                s = jnp.where(ok, s, -jnp.inf)
                top = jnp.max(s, axis=1, keepdims=True)
                if not first:
                    before = ms[r, 0:1]
                    top = jnp.maximum(before, top)
                    keep = jnp.exp2((before - top) * factor)
                p = jnp.exp2((s - top) * factor)
                total = jnp.sum(p, axis=1, keepdims=True)
                o = jnp.dot(p.astype(jnp.bfloat16), vv, preferred_element_type=jnp.float32)
                if not first:
                    total = keep * ls[r, 0:1] + total
                    o = keep * acc[r, :] + o
                ms[r, :] = jnp.broadcast_to(top, (tall, HD))
                ls[r, :] = jnp.broadcast_to(total, (tall, HD))
                acc[r, :] = o

        step(0, True)

        def body(t, c):
            step(t, False)
            return c

        lax.fori_loop(1, lax.div(n + (SPAN - 1), jnp.int32(SPAN)), body, 0)
        for h in range(hq):
            r = slice(h * BLOCK, (h + 1) * BLOCK)
            out[rows, h * HD:(h + 1) * HD] = (acc[r, :] / ls[r, :]).astype(jnp.bfloat16)
        return carry

    lax.fori_loop(0, blocks, one_block, 0)


def attend(query_ids, key_ids, queries, stacked, others):
    rows, cols = queries.shape
    tall = cols // HD * BLOCK
    room = rows * (ROUNDS + 1) + SPAN * BLOCK
    smem = pl.BlockSpec(memory_space=pltpu.SMEM)
    vmem = pl.BlockSpec(memory_space=pltpu.VMEM)
    return pl.pallas_call(
        attend_kernel,
        out_shape=jax.ShapeDtypeStruct(queries.shape, queries.dtype),
        in_specs=[smem, smem] + [vmem] * 3,
        out_specs=vmem,
        scratch_shapes=[pltpu.VMEM((room, HD), jnp.bfloat16)] * 2
        + [pltpu.VMEM((tall, HD), jnp.bfloat16)]
        + [pltpu.VMEM((tall, HD), jnp.float32)] * 3,
        compiler_params=pltpu.CompilerParams(vmem_limit_bytes=24 << 20),
        cost_estimate=pl.CostEstimate(flops=2 * rows * rows * 4 * cols * 2, bytes_accessed=4 << 20, transcendentals=rows * rows * 32),
    )(query_ids, key_ids, queries, stacked, others)


def project_kernel(info, a0, a1, a2, a3, w, out):
    total = None
    for step, a in enumerate((a0, a1, a2, a3)):
        term = jnp.dot(a[...], w[info[1 + step], 0], preferred_element_type=jnp.float32)
        total = term if total is None else total + term
    out[...] = total.astype(jnp.bfloat16)


def project(info, attn, weight, start, count):
    rows, depth = attn[0].shape
    cols = weight.shape[3]
    whole = pl.BlockSpec((rows, depth), lambda j, info: (0, 0))
    return pl.pallas_call(
        project_kernel,
        out_shape=jax.ShapeDtypeStruct((rows, count * cols), jnp.bfloat16),
        grid_spec=pltpu.PrefetchScalarGridSpec(
            num_scalar_prefetch=1,
            grid=(count,),
            in_specs=[whole] * 4 + [pl.BlockSpec((4, 1, depth, cols), lambda j, info: (0, info[start] + j, 0, 0))],
            out_specs=pl.BlockSpec((rows, cols), lambda j, info: (0, j)),
        ),
        compiler_params=pltpu.CompilerParams(vmem_limit_bytes=52 << 20),
        cost_estimate=pl.CostEstimate(flops=2 * rows * depth * 4 * cols * count, bytes_accessed=12 << 20, transcendentals=0),
    )(info, *attn, weight)


def first_kernel(info, attn, w, up, down):
    a = attn[...]
    cols = w.shape[3]
    for x in range(4):
        out = (up, down)[x // 2]
        at = x % 2 * cols
        out[:, at:at + cols] = jnp.dot(a, w[info[2], x], preferred_element_type=jnp.float32).astype(jnp.bfloat16)


def rest_kernel(info, attn, w, up, down, own):
    a = attn[...]
    cols = w.shape[3]
    for step, out in ((1, up), (3, down), (0, own)):
        for x in range(4):
            at = x * cols
            out[:, at:at + cols] = jnp.dot(a, w[info[step], x], preferred_element_type=jnp.float32).astype(jnp.bfloat16)


def pieces(kernel, info, attn, weight, widths):
    rows, depth = attn.shape
    smem = pl.BlockSpec(memory_space=pltpu.SMEM)
    vmem = pl.BlockSpec(memory_space=pltpu.VMEM)
    return pl.pallas_call(
        kernel,
        out_shape=[jax.ShapeDtypeStruct((rows, width), jnp.bfloat16) for width in widths],
        in_specs=[smem, vmem, vmem],
        out_specs=[vmem] * len(widths),
        compiler_params=pltpu.CompilerParams(vmem_limit_bytes=24 << 20),
        cost_estimate=pl.CostEstimate(flops=2 * rows * depth * sum(widths), bytes_accessed=10 << 20, transcendentals=0),
    )(info, attn, weight)


def reduce_y(info, attn, weight):
    cols = 2 * weight.shape[3]
    up2, down2 = pieces(first_kernel, info, attn, weight, (cols, cols))
    a, b = to_y(up2, 1), to_y(down2, -1)
    up, down, own = pieces(rest_kernel, info, attn, weight, (2 * cols,) * 3)
    up = jnp.concatenate([add(up[:, :cols], a), up[:, cols:]], axis=1)
    down = jnp.concatenate([down[:, :cols], add(down[:, cols:], b)], axis=1)
    return own, to_y(up, 1), to_y(down, -1)


def add(*terms):
    total = terms[0].astype(jnp.float32)
    for term in terms[1:]:
        total = total + term.astype(jnp.float32)
    return total.astype(jnp.bfloat16)


def gather_y(attn):
    half = attn.shape[1] // 2
    below = to_y(attn, 1)
    above = to_y(attn, -1)
    left = to_y(below[:, :half], 1)
    right = to_y(above[:, half:], -1)
    return [attn, above, jnp.concatenate([left, right], axis=1), below]


def local(queries, key_states, values, out_weight, pair_table, block_order):
    rank = lax.axis_index("ctx")
    head = lax.axis_index("head")
    y, low = head // 2, head % 2
    core = rank % 2
    depth, cols = out_weight.shape

    upper, lower = out_weight[:depth // 2], out_weight[depth // 2:]
    mine = jnp.where(core == 0, upper, lower)
    swapped = from_sibling(jnp.where(core == 0, lower, upper))
    first = lax.all_gather(jnp.where(core == 0, mine, swapped), "ctx", axis=0)
    first = first.reshape((4, 4, depth, cols))
    moved = jnp.where(core == 0, swapped, mine)

    stacked = jnp.stack((key_states, values))
    masks = pair_table[:, 0]
    others = lax.map(lambda m: exchange(stacked, m), masks)
    moved, others = lax.optimization_barrier((moved, others))
    moved = transpose_yz(moved)

    blk_dev = queries.shape[0] // BLOCK

    def ids(r):
        return lax.dynamic_slice_in_dim(block_order, r * blk_dev, blk_dev, 0)

    query_ids = ids(rank)
    key_ids = jnp.concatenate([query_ids] + [ids(jnp.bitwise_xor(rank, masks[i])) for i in range(ROUNDS)])
    attn = attend(query_ids, key_ids, queries, stacked, others)
    moved, attn = lax.optimization_barrier((moved, attn))
    second = lax.all_gather(moved, "ctx", axis=0)
    second = second.reshape((4, 4, depth, cols))
    gathered = gather_y(attn)

    groups = ((y + jnp.arange(4, dtype=jnp.int32)) % 4).astype(jnp.int32)
    gathered, attn, groups = lax.optimization_barrier((gathered, attn, groups))
    terms = reduce_y(groups, attn, first)
    half = 2 * cols

    def side(arr, s):
        return jnp.where(s == 0, arr[:, :half], arr[:, half:])

    sent = add(*[side(t, 1 - low) for t in terms])
    sent, gathered = lax.optimization_barrier((sent, gathered))
    core0 = add(*[side(t, low) for t in terms], swap_low(sent))

    info = jnp.concatenate([jnp.zeros((1,), jnp.int32), groups, jnp.stack([2 * (1 - low), 2 * low]).astype(jnp.int32)])
    arrived = swap_low(project(info, gathered, second, 5, 2))
    core1 = add(project(info, gathered, second, 6, 2), arrived)
    return jnp.concatenate([core0[:, :cols], core1[:, :cols], core0[:, cols:], core1[:, cols:]], axis=1)


def solution(mesh):
    in_specs = (P("ctx", "head"), P("ctx", "head"), P("ctx", "head"), P("head", "ctx"), P(), P())
    return jax.shard_map(local, mesh=mesh, in_specs=in_specs, out_specs=P("ctx", "head"), check_vma=False)
```

```python
import math

import jax
import jax.numpy as jnp
from jax import lax
from jax.experimental import pallas as pl
from jax.experimental.pallas import tpu as pltpu
from jax.sharding import PartitionSpec as P

HD = 128
BLOCK = 128
ROUNDS = 3
SPAN = 4
GROUP = 2

CTX = [(z, x, c) for z in range(4) for x in range(4) for c in range(2)]
HEAD = [(y, s) for y in range(4) for s in range(2)]


def ctx_pairs(place):
    pairs = []
    for here in CTX:
        z, x, c = place(*here)
        pairs.append((here[0] * 8 + here[1] * 2 + here[2], z % 4 * 8 + x % 4 * 2 + c))
    return pairs


def head_pairs(place):
    pairs = []
    for here in HEAD:
        y, s = place(*here)
        pairs.append((here[0] * 2 + here[1], y % 4 * 2 + s))
    return pairs


def transpose_yz(arr):
    pairs = []
    for y, s in HEAD:
        for z, x, c in CTX:
            here = (y * 2 + s) * 32 + z * 8 + x * 2 + c
            pairs.append((here, (z * 2 + s) * 32 + y * 8 + x * 2 + c))
    return lax.ppermute(arr, ("head", "ctx"), pairs)


def from_sibling(arr):
    return lax.ppermute(arr, "ctx", ctx_pairs(lambda z, x, c: (z, x, 1 - c)))


def to_y(arr, step):
    return lax.ppermute(arr, "head", head_pairs(lambda y, s: (y + step, s)))


def swap_low(arr):
    return lax.ppermute(arr, "head", head_pairs(lambda y, s: (y, 1 - s)))


def exchange(stacked, mask):
    ranks = len(CTX)

    def branch(m):
        return lambda arr: lax.ppermute(arr, "ctx", [(i, i ^ m) for i in range(ranks)])

    return lax.switch(mask - 1, [branch(m) for m in range(1, ranks)], stacked)


def attend_kernel(qid, kid, q_ref, kv0, others, out, kc, vc, qs, ms, ls, acc):
    srcs = [kv0] + [others.at[i] for i in range(ROUNDS)]
    hq = q_ref.shape[1] // HD
    blocks = q_ref.shape[0] // BLOCK
    factor = HD ** -0.5 * math.log2(math.e)
    width = SPAN * BLOCK
    tall = GROUP * BLOCK
    vc[...] = jnp.zeros_like(vc)

    def one_block(i, carry):
        me = qid[i]
        rows = pl.ds(pl.multiple_of(i * BLOCK, BLOCK), BLOCK)
        kc[0:BLOCK, :] = kv0[0, rows, :]
        vc[0:BLOCK, :] = kv0[1, rows, :]
        n = jnp.int32(1)
        for j in range(blocks * (ROUNDS + 1)):
            take = kid[j] < me
            src = srcs[j // blocks]
            lo = j % blocks * BLOCK

            @pl.when(take)
            def _():
                dst = pl.ds(pl.multiple_of(n * BLOCK, BLOCK), BLOCK)
                kc[dst, :] = src[0, lo:lo + BLOCK, :]
                vc[dst, :] = src[1, lo:lo + BLOCK, :]

            n = n + take.astype(jnp.int32)
        for h in range(hq):
            qs[h * BLOCK:(h + 1) * BLOCK, :] = q_ref[rows, h * HD:(h + 1) * HD]

        def step(t, first):
            base = pl.multiple_of(t * width, width)
            kk = kc[pl.ds(base, width), :]
            vv = vc[pl.ds(base, width), :]
            col = lax.broadcasted_iota(jnp.int32, (tall, width), 1)
            if first:
                row = lax.broadcasted_iota(jnp.int32, (tall, width), 0) & (BLOCK - 1)
                ok = (col <= row) | ((col >= BLOCK) & (col < n * BLOCK))
            else:
                ok = col < n * BLOCK - base
            for g in range(hq // GROUP):
                r = slice(g * tall, (g + 1) * tall)
                s = lax.dot_general(qs[r, :], kk, (((1,), (1,)), ((), ())), preferred_element_type=jnp.float32)
                s = jnp.where(ok, s, -jnp.inf)
                top = jnp.max(s, axis=1, keepdims=True)
                if not first:
                    before = ms[r, 0:1]
                    top = jnp.maximum(before, top)
                    keep = jnp.exp2((before - top) * factor)
                p = jnp.exp2((s - top) * factor)
                total = jnp.sum(p, axis=1, keepdims=True)
                o = jnp.dot(p.astype(jnp.bfloat16), vv, preferred_element_type=jnp.float32)
                if not first:
                    total = keep * ls[r, 0:1] + total
                    o = keep * acc[r, :] + o
                ms[r, :] = jnp.broadcast_to(top, (tall, HD))
                ls[r, :] = jnp.broadcast_to(total, (tall, HD))
                acc[r, :] = o

        step(0, True)

        def body(t, c):
            step(t, False)
            return c

        lax.fori_loop(1, lax.div(n + (SPAN - 1), jnp.int32(SPAN)), body, 0)
        for h in range(hq):
            r = slice(h * BLOCK, (h + 1) * BLOCK)
            out[rows, h * HD:(h + 1) * HD] = (acc[r, :] / ls[r, :]).astype(jnp.bfloat16)
        return carry

    lax.fori_loop(0, blocks, one_block, 0)


def attend(query_ids, key_ids, queries, stacked, others):
    rows, cols = queries.shape
    tall = cols // HD * BLOCK
    room = rows * (ROUNDS + 1) + SPAN * BLOCK
    smem = pl.BlockSpec(memory_space=pltpu.SMEM)
    vmem = pl.BlockSpec(memory_space=pltpu.VMEM)
    return pl.pallas_call(
        attend_kernel,
        out_shape=jax.ShapeDtypeStruct(queries.shape, queries.dtype),
        in_specs=[smem, smem] + [vmem] * 3,
        out_specs=vmem,
        scratch_shapes=[pltpu.VMEM((room, HD), jnp.bfloat16)] * 2
        + [pltpu.VMEM((tall, HD), jnp.bfloat16)]
        + [pltpu.VMEM((tall, HD), jnp.float32)] * 3,
        compiler_params=pltpu.CompilerParams(vmem_limit_bytes=24 << 20),
        cost_estimate=pl.CostEstimate(flops=2 * rows * rows * 4 * cols * 2, bytes_accessed=4 << 20, transcendentals=rows * rows * 32),
    )(query_ids, key_ids, queries, stacked, others)


def project_kernel(info, a0, a1, a2, a3, w, out):
    total = None
    for step, a in enumerate((a0, a1, a2, a3)):
        term = jnp.dot(a[...], w[info[1 + step], 0], preferred_element_type=jnp.float32)
        total = term if total is None else total + term
    out[...] = total.astype(jnp.bfloat16)


def project(info, attn, weight, start, count):
    rows, depth = attn[0].shape
    cols = weight.shape[3]
    whole = pl.BlockSpec(memory_space=pltpu.VMEM)
    return pl.pallas_call(
        project_kernel,
        out_shape=jax.ShapeDtypeStruct((rows, count * cols), jnp.bfloat16),
        grid_spec=pltpu.PrefetchScalarGridSpec(
            num_scalar_prefetch=1,
            grid=(count,),
            in_specs=[whole] * 4 + [pl.BlockSpec((4, 1, depth, cols), lambda j, info: (0, info[start] + j, 0, 0))],
            out_specs=pl.BlockSpec((rows, cols), lambda j, info: (0, j)),
        ),
        compiler_params=pltpu.CompilerParams(vmem_limit_bytes=52 << 20),
        cost_estimate=pl.CostEstimate(flops=2 * rows * depth * 4 * cols * count, bytes_accessed=12 << 20, transcendentals=0),
    )(info, *attn, weight)


def first_kernel(info, attn, w, up, down):
    a = attn[...]
    cols = w.shape[3]
    for x in range(4):
        out = (up, down)[x // 2]
        at = x % 2 * cols
        out[:, at:at + cols] = jnp.dot(a, w[info[2], x], preferred_element_type=jnp.float32).astype(jnp.bfloat16)


def rest_kernel(info, attn, w, up, down, own):
    a = attn[...]
    cols = w.shape[3]
    for step, out in ((1, up), (3, down), (0, own)):
        for x in range(4):
            at = x * cols
            out[:, at:at + cols] = jnp.dot(a, w[info[step], x], preferred_element_type=jnp.float32).astype(jnp.bfloat16)


def pieces(kernel, info, attn, weight, widths):
    rows, depth = attn.shape
    smem = pl.BlockSpec(memory_space=pltpu.SMEM)
    vmem = pl.BlockSpec(memory_space=pltpu.VMEM)
    return pl.pallas_call(
        kernel,
        out_shape=[jax.ShapeDtypeStruct((rows, width), jnp.bfloat16) for width in widths],
        in_specs=[smem, vmem, vmem],
        out_specs=[vmem] * len(widths),
        compiler_params=pltpu.CompilerParams(vmem_limit_bytes=24 << 20),
        cost_estimate=pl.CostEstimate(flops=2 * rows * depth * sum(widths), bytes_accessed=10 << 20, transcendentals=0),
    )(info, attn, weight)


def reduce_y(info, attn, weight):
    cols = 2 * weight.shape[3]
    up2, down2 = pieces(first_kernel, info, attn, weight, (cols, cols))
    a, b = to_y(up2, 1), to_y(down2, -1)
    up, down, own = pieces(rest_kernel, info, attn, weight, (2 * cols,) * 3)
    up = jnp.concatenate([add(up[:, :cols], a), up[:, cols:]], axis=1)
    down = jnp.concatenate([down[:, :cols], add(down[:, cols:], b)], axis=1)
    return own, to_y(up, 1), to_y(down, -1)


def add(*terms):
    total = terms[0].astype(jnp.float32)
    for term in terms[1:]:
        total = total + term.astype(jnp.float32)
    return total.astype(jnp.bfloat16)


def gather_y(attn):
    half = attn.shape[1] // 2
    below = to_y(attn, 1)
    above = to_y(attn, -1)
    left = to_y(below[:, :half], 1)
    right = to_y(above[:, half:], -1)
    return [attn, above, jnp.concatenate([left, right], axis=1), below]


def local(queries, key_states, values, out_weight, pair_table, block_order):
    rank = lax.axis_index("ctx")
    head = lax.axis_index("head")
    y, low = head // 2, head % 2
    core = rank % 2
    depth, cols = out_weight.shape

    upper, lower = out_weight[:depth // 2], out_weight[depth // 2:]
    mine = jnp.where(core == 0, upper, lower)
    swapped = from_sibling(jnp.where(core == 0, lower, upper))
    first = jnp.where(core == 0, mine, swapped)
    moved = jnp.where(core == 0, swapped, mine)

    stacked = jnp.stack((key_states, values))
    masks = pair_table[:, 0]
    others = lax.map(lambda m: exchange(stacked, m), masks)
    first, moved, others = lax.optimization_barrier((first, moved, others))
    first = lax.all_gather(first, "ctx", axis=0).reshape((4, 4, depth, cols))
    moved = transpose_yz(moved)

    blk_dev = queries.shape[0] // BLOCK

    def ids(r):
        return lax.dynamic_slice_in_dim(block_order, r * blk_dev, blk_dev, 0)

    query_ids = ids(rank)
    key_ids = jnp.concatenate([query_ids] + [ids(jnp.bitwise_xor(rank, masks[i])) for i in range(ROUNDS)])
    attn = attend(query_ids, key_ids, queries, stacked, others)
    moved, attn = lax.optimization_barrier((moved, attn))
    second = lax.all_gather(moved, "ctx", axis=0)
    second = second.reshape((4, 4, depth, cols))
    gathered = gather_y(attn)

    groups = ((y + jnp.arange(4, dtype=jnp.int32)) % 4).astype(jnp.int32)
    gathered, attn, groups = lax.optimization_barrier((gathered, attn, groups))
    terms = reduce_y(groups, attn, first)
    half = 2 * cols

    def side(arr, s):
        return jnp.where(s == 0, arr[:, :half], arr[:, half:])

    sent = add(*[side(t, 1 - low) for t in terms])
    sent, gathered = lax.optimization_barrier((sent, gathered))
    core0 = add(*[side(t, low) for t in terms], swap_low(sent))

    info = jnp.concatenate([jnp.zeros((1,), jnp.int32), groups, jnp.stack([2 * (1 - low), 2 * low]).astype(jnp.int32)])
    arrived = swap_low(project(info, gathered, second, 5, 2))
    core1 = add(project(info, gathered, second, 6, 2), arrived)
    return jnp.concatenate([core0[:, :cols], core1[:, :cols], core0[:, cols:], core1[:, cols:]], axis=1)


def solution(mesh):
    in_specs = (P("ctx", "head"), P("ctx", "head"), P("ctx", "head"), P("head", "ctx"), P(), P())
    return jax.shard_map(local, mesh=mesh, in_specs=in_specs, out_specs=P("ctx", "head"), check_vma=False)
```

```python
import math

import jax
import jax.numpy as jnp
from jax import lax
from jax.experimental import pallas as pl
from jax.experimental.pallas import tpu as pltpu
from jax.sharding import PartitionSpec as P

HD = 128
BLOCK = 128
ROUNDS = 3
SPAN = 4
GROUP = 2

CTX = [(z, x, c) for z in range(4) for x in range(4) for c in range(2)]
HEAD = [(y, s) for y in range(4) for s in range(2)]


def ctx_pairs(place):
    pairs = []
    for here in CTX:
        z, x, c = place(*here)
        pairs.append((here[0] * 8 + here[1] * 2 + here[2], z % 4 * 8 + x % 4 * 2 + c))
    return pairs


def head_pairs(place):
    pairs = []
    for here in HEAD:
        y, s = place(*here)
        pairs.append((here[0] * 2 + here[1], y % 4 * 2 + s))
    return pairs


def transpose_yz(arr):
    pairs = []
    for y, s in HEAD:
        for z, x, c in CTX:
            here = (y * 2 + s) * 32 + z * 8 + x * 2 + c
            pairs.append((here, (z * 2 + s) * 32 + y * 8 + x * 2 + c))
    return lax.ppermute(arr, ("head", "ctx"), pairs)


def to_y(arr, step):
    return lax.ppermute(arr, "head", head_pairs(lambda y, s: (y + step, s)))


def swap_low(arr):
    return lax.ppermute(arr, "head", head_pairs(lambda y, s: (y, 1 - s)))


def exchange(arr, mask, shift, bits):
    def branch(m):
        return lambda held: lax.ppermute(held, "ctx", [(i, i ^ (m << shift)) for i in range(len(CTX))])

    return lax.switch(mask, [lambda held: held] + [branch(m) for m in range(1, 1 << bits)], arr)


def attend_kernel(qid, kid, q_ref, kv0, kv1, kv2, kv3, out, kc, vc, qs, ms, ls, acc):
    srcs = (kv0, kv1, kv2, kv3)
    hq = q_ref.shape[1] // HD
    blocks = q_ref.shape[0] // BLOCK
    factor = HD ** -0.5 * math.log2(math.e)
    width = SPAN * BLOCK
    tall = GROUP * BLOCK
    vc[...] = jnp.zeros_like(vc)

    def one_block(i, carry):
        me = qid[i]
        rows = pl.ds(pl.multiple_of(i * BLOCK, BLOCK), BLOCK)
        kc[0:BLOCK, :] = kv0[0, rows, :]
        vc[0:BLOCK, :] = kv0[1, rows, :]
        n = jnp.int32(1)
        for j in range(blocks * (ROUNDS + 1)):
            take = kid[j] < me
            src = srcs[j // blocks]
            lo = j % blocks * BLOCK

            @pl.when(take)
            def _():
                dst = pl.ds(pl.multiple_of(n * BLOCK, BLOCK), BLOCK)
                kc[dst, :] = src[0, lo:lo + BLOCK, :]
                vc[dst, :] = src[1, lo:lo + BLOCK, :]

            n = n + take.astype(jnp.int32)
        for h in range(hq):
            qs[h * BLOCK:(h + 1) * BLOCK, :] = q_ref[rows, h * HD:(h + 1) * HD]

        def step(t, first):
            base = pl.multiple_of(t * width, width)
            kk = kc[pl.ds(base, width), :]
            vv = vc[pl.ds(base, width), :]
            col = lax.broadcasted_iota(jnp.int32, (tall, width), 1)
            if first:
                row = lax.broadcasted_iota(jnp.int32, (tall, width), 0) & (BLOCK - 1)
                ok = (col <= row) | ((col >= BLOCK) & (col < n * BLOCK))
            else:
                ok = col < n * BLOCK - base
            for g in range(hq // GROUP):
                r = slice(g * tall, (g + 1) * tall)
                s = lax.dot_general(qs[r, :], kk, (((1,), (1,)), ((), ())), preferred_element_type=jnp.float32)
                s = jnp.where(ok, s, -jnp.inf)
                top = jnp.max(s, axis=1, keepdims=True)
                if not first:
                    before = ms[r, 0:1]
                    top = jnp.maximum(before, top)
                    keep = jnp.exp2((before - top) * factor)
                p = jnp.exp2((s - top) * factor)
                total = jnp.sum(p, axis=1, keepdims=True)
                o = jnp.dot(p.astype(jnp.bfloat16), vv, preferred_element_type=jnp.float32)
                if not first:
                    total = keep * ls[r, 0:1] + total
                    o = keep * acc[r, :] + o
                ms[r, :] = jnp.broadcast_to(top, (tall, HD))
                ls[r, :] = jnp.broadcast_to(total, (tall, HD))
                acc[r, :] = o

        step(0, True)

        def body(t, c):
            step(t, False)
            return c

        lax.fori_loop(1, lax.div(n + (SPAN - 1), jnp.int32(SPAN)), body, 0)
        for h in range(hq):
            r = slice(h * BLOCK, (h + 1) * BLOCK)
            out[rows, h * HD:(h + 1) * HD] = (acc[r, :] / ls[r, :]).astype(jnp.bfloat16)
        return carry

    lax.fori_loop(0, blocks, one_block, 0)


def attend(query_ids, key_ids, queries, kv_list):
    rows, cols = queries.shape
    tall = cols // HD * BLOCK
    room = rows * (ROUNDS + 1) + SPAN * BLOCK
    smem = pl.BlockSpec(memory_space=pltpu.SMEM)
    vmem = pl.BlockSpec(memory_space=pltpu.VMEM)
    return pl.pallas_call(
        attend_kernel,
        out_shape=jax.ShapeDtypeStruct(queries.shape, queries.dtype),
        in_specs=[smem, smem] + [vmem] * 5,
        out_specs=vmem,
        scratch_shapes=[pltpu.VMEM((room, HD), jnp.bfloat16)] * 2
        + [pltpu.VMEM((tall, HD), jnp.bfloat16)]
        + [pltpu.VMEM((tall, HD), jnp.float32)] * 3,
        compiler_params=pltpu.CompilerParams(vmem_limit_bytes=24 << 20),
        cost_estimate=pl.CostEstimate(flops=2 * rows * rows * 4 * cols * 2, bytes_accessed=4 << 20, transcendentals=rows * rows * 32),
    )(query_ids, key_ids, queries, *kv_list)


def project_kernel(info, a0, a1, a2, a3, w, out):
    total = None
    for step, a in enumerate((a0, a1, a2, a3)):
        term = jnp.dot(a[...], w[info[1 + step], 0], preferred_element_type=jnp.float32)
        total = term if total is None else total + term
    out[...] = total.astype(jnp.bfloat16)


def project(info, attn, weight, start, count):
    rows, depth = attn[0].shape
    cols = weight.shape[3]
    whole = pl.BlockSpec(memory_space=pltpu.VMEM)
    return pl.pallas_call(
        project_kernel,
        out_shape=jax.ShapeDtypeStruct((rows, count * cols), jnp.bfloat16),
        grid_spec=pltpu.PrefetchScalarGridSpec(
            num_scalar_prefetch=1,
            grid=(count,),
            in_specs=[whole] * 4 + [pl.BlockSpec((4, 1, depth, cols), lambda j, info: (0, info[start] + j, 0, 0))],
            out_specs=pl.BlockSpec((rows, cols), lambda j, info: (0, j)),
        ),
        compiler_params=pltpu.CompilerParams(vmem_limit_bytes=48 << 20),
        cost_estimate=pl.CostEstimate(flops=2 * rows * depth * 4 * cols * count, bytes_accessed=12 << 20, transcendentals=0),
    )(info, *attn, weight)


def add(*terms):
    total = terms[0].astype(jnp.float32)
    for term in terms[1:]:
        total = total + term.astype(jnp.float32)
    return total.astype(jnp.bfloat16)


def gather_y(attn):
    half = attn.shape[1] // 2
    below = to_y(attn, 1)
    above = to_y(attn, -1)
    left = to_y(below[:, :half], 1)
    right = to_y(above[:, half:], -1)
    return [attn, above, jnp.concatenate([left, right], axis=1), below]


def local(queries, key_states, values, out_weight, pair_table, block_order):
    rank = lax.axis_index("ctx")
    head = lax.axis_index("head")
    y, low = head // 2, head % 2

    moved = transpose_yz(out_weight)
    stacked = jnp.stack((key_states, values))
    masks = [pair_table[i, 0] for i in range(ROUNDS)]
    near = [exchange(stacked, mask & 7, 0, 3) for mask in masks]
    moved, near = lax.optimization_barrier((moved, near))
    weight = lax.all_gather(moved, "ctx", axis=0)
    weight = weight.reshape((4, 8) + out_weight.shape)
    kv_list = [stacked] + [exchange(arr, mask >> 3, 3, 2) for arr, mask in zip(near, masks)]

    blk_dev = queries.shape[0] // BLOCK

    def ids(r):
        return lax.dynamic_slice_in_dim(block_order, r * blk_dev, blk_dev, 0)

    query_ids = ids(rank)
    key_ids = jnp.concatenate([query_ids] + [ids(jnp.bitwise_xor(rank, masks[i])) for i in range(ROUNDS)])
    attn = gather_y(attend(query_ids, key_ids, queries, kv_list))

    steps = jnp.arange(4, dtype=jnp.int32)
    sent, kept = 4 * (1 - low), 4 * low
    starts = jnp.stack([sent, sent + 2, kept])
    info = jnp.concatenate([jnp.zeros((1,), jnp.int32), (y + steps) % 4, starts]).astype(jnp.int32)
    arrived = [swap_low(project(info, attn, weight, 5 + i, 2)) for i in range(2)]
    ours = project(info, attn, weight, 7, 4)
    return add(ours, jnp.concatenate(arrived, axis=1))


def solution(mesh):
    in_specs = (P("ctx", "head"), P("ctx", "head"), P("ctx", "head"), P("head", "ctx"), P(), P())
    return jax.shard_map(local, mesh=mesh, in_specs=in_specs, out_specs=P("ctx", "head"), check_vma=False)
```

```python
import math

import jax
import jax.numpy as jnp
from jax import lax
from jax.experimental import pallas as pl
from jax.experimental.pallas import tpu as pltpu
from jax.sharding import PartitionSpec as P

HD = 128
BLOCK = 128
ROUNDS = 3
SPAN = 4
GROUP = 2

CTX = [(z, x, c) for z in range(4) for x in range(4) for c in range(2)]
HEAD = [(y, s) for y in range(4) for s in range(2)]


def ctx_pairs(place):
    pairs = []
    for here in CTX:
        z, x, c = place(*here)
        pairs.append((here[0] * 8 + here[1] * 2 + here[2], z % 4 * 8 + x % 4 * 2 + c))
    return pairs


def head_pairs(place):
    pairs = []
    for here in HEAD:
        y, s = place(*here)
        pairs.append((here[0] * 2 + here[1], y % 4 * 2 + s))
    return pairs


def gather_z(arr):
    groups = [[z * 8 + x * 2 + c for z in range(4)] for x in range(4) for c in range(2)]
    return lax.all_gather(arr, "ctx", axis_index_groups=groups, axis=0)


def to_x(arr, step):
    return lax.ppermute(arr, "ctx", ctx_pairs(lambda z, x, c: (z, x + step, c)))


def from_sibling(arr):
    return lax.ppermute(arr, "ctx", ctx_pairs(lambda z, x, c: (z, x, 1 - c)))


def to_y(arr, step):
    return lax.ppermute(arr, "head", head_pairs(lambda y, s: (y + step, s)))


def swap_low(arr):
    return lax.ppermute(arr, "head", head_pairs(lambda y, s: (y, 1 - s)))


def exchange(arr, mask, shift, bits):
    def branch(m):
        return lambda held: lax.ppermute(held, "ctx", [(i, i ^ (m << shift)) for i in range(len(CTX))])

    return lax.switch(mask, [lambda held: held] + [branch(m) for m in range(1, 1 << bits)], arr)


def attend_kernel(qid, kid, q_ref, kv0, kv1, kv2, kv3, out, kc, vc, qs, ms, ls, acc):
    srcs = (kv0, kv1, kv2, kv3)
    hq = q_ref.shape[1] // HD
    blocks = q_ref.shape[0] // BLOCK
    factor = HD ** -0.5 * math.log2(math.e)
    width = SPAN * BLOCK
    tall = GROUP * BLOCK
    vc[...] = jnp.zeros_like(vc)

    def one_block(i, carry):
        me = qid[i]
        rows = pl.ds(pl.multiple_of(i * BLOCK, BLOCK), BLOCK)
        kc[0:BLOCK, :] = kv0[0, rows, :]
        vc[0:BLOCK, :] = kv0[1, rows, :]
        n = jnp.int32(1)
        for j in range(blocks * (ROUNDS + 1)):
            take = kid[j] < me
            src = srcs[j // blocks]
            lo = j % blocks * BLOCK

            @pl.when(take)
            def _():
                dst = pl.ds(pl.multiple_of(n * BLOCK, BLOCK), BLOCK)
                kc[dst, :] = src[0, lo:lo + BLOCK, :]
                vc[dst, :] = src[1, lo:lo + BLOCK, :]

            n = n + take.astype(jnp.int32)
        for h in range(hq):
            qs[h * BLOCK:(h + 1) * BLOCK, :] = q_ref[rows, h * HD:(h + 1) * HD]

        def step(t, first):
            base = pl.multiple_of(t * width, width)
            kk = kc[pl.ds(base, width), :]
            vv = vc[pl.ds(base, width), :]
            col = lax.broadcasted_iota(jnp.int32, (tall, width), 1)
            if first:
                row = lax.broadcasted_iota(jnp.int32, (tall, width), 0) & (BLOCK - 1)
                ok = (col <= row) | ((col >= BLOCK) & (col < n * BLOCK))
            else:
                ok = col < n * BLOCK - base
            for g in range(hq // GROUP):
                r = slice(g * tall, (g + 1) * tall)
                s = lax.dot_general(qs[r, :], kk, (((1,), (1,)), ((), ())), preferred_element_type=jnp.float32)
                s = jnp.where(ok, s, -jnp.inf)
                top = jnp.max(s, axis=1, keepdims=True)
                if not first:
                    before = ms[r, 0:1]
                    top = jnp.maximum(before, top)
                    keep = jnp.exp2((before - top) * factor)
                p = jnp.exp2((s - top) * factor)
                total = jnp.sum(p, axis=1, keepdims=True)
                o = jnp.dot(p.astype(jnp.bfloat16), vv, preferred_element_type=jnp.float32)
                if not first:
                    total = keep * ls[r, 0:1] + total
                    o = keep * acc[r, :] + o
                ms[r, :] = jnp.broadcast_to(top, (tall, HD))
                ls[r, :] = jnp.broadcast_to(total, (tall, HD))
                acc[r, :] = o

        step(0, True)

        def body(t, c):
            step(t, False)
            return c

        lax.fori_loop(1, lax.div(n + (SPAN - 1), jnp.int32(SPAN)), body, 0)
        for h in range(hq):
            r = slice(h * BLOCK, (h + 1) * BLOCK)
            out[rows, h * HD:(h + 1) * HD] = (acc[r, :] / ls[r, :]).astype(jnp.bfloat16)
        return carry

    lax.fori_loop(0, blocks, one_block, 0)


def attend(query_ids, key_ids, queries, kv_list):
    rows, cols = queries.shape
    tall = cols // HD * BLOCK
    room = rows * (ROUNDS + 1) + SPAN * BLOCK
    smem = pl.BlockSpec(memory_space=pltpu.SMEM)
    vmem = pl.BlockSpec(memory_space=pltpu.VMEM)
    return pl.pallas_call(
        attend_kernel,
        out_shape=jax.ShapeDtypeStruct(queries.shape, queries.dtype),
        in_specs=[smem, smem] + [vmem] * 5,
        out_specs=vmem,
        scratch_shapes=[pltpu.VMEM((room, HD), jnp.bfloat16)] * 2
        + [pltpu.VMEM((tall, HD), jnp.bfloat16)]
        + [pltpu.VMEM((tall, HD), jnp.float32)] * 3,
        compiler_params=pltpu.CompilerParams(vmem_limit_bytes=24 << 20),
        cost_estimate=pl.CostEstimate(flops=2 * rows * rows * 4 * cols * 2, bytes_accessed=4 << 20, transcendentals=rows * rows * 32),
    )(query_ids, key_ids, queries, *kv_list)


def project_kernel(info, a0, a1, a2, a3, *refs):
    one, other, sent, kept = refs[0:2], refs[2:4], refs[-2], refs[-1]
    core, one_sent = info[0], info[1]
    near_at = pl.ds(pl.multiple_of(core * 256, 256), 256)
    far_at = pl.ds(pl.multiple_of((1 - core) * 256, 256), 256)

    def product(weights, out):
        for w, at in zip(weights, (near_at, far_at)):
            total = None
            for step, a in enumerate((a0, a1, a2, a3)):
                term = jnp.dot(a[...], w[step], preferred_element_type=jnp.float32)
                total = term if total is None else total + term
            out[:, at] = total.astype(jnp.bfloat16)

    first = one_sent == 1

    @pl.when(first)
    def _():
        product(one, sent)
        product(other, kept)

    @pl.when(jnp.logical_not(first))
    def _():
        product(other, sent)
        product(one, kept)


def project(core, one_sent, attn, one, other):
    rows, depth = attn[0].shape
    cols = one[0].shape[2]
    smem = pl.BlockSpec(memory_space=pltpu.SMEM)
    vmem = pl.BlockSpec(memory_space=pltpu.VMEM)
    info = jnp.stack([core, one_sent.astype(jnp.int32)])
    return pl.pallas_call(
        project_kernel,
        out_shape=(jax.ShapeDtypeStruct((rows, 2 * cols), jnp.bfloat16),) * 2,
        in_specs=[smem] + [vmem] * 8,
        out_specs=(vmem,) * 2,
        compiler_params=pltpu.CompilerParams(vmem_limit_bytes=24 << 20),
        cost_estimate=pl.CostEstimate(flops=2 * rows * depth * 4 * cols * 4, bytes_accessed=13 << 20, transcendentals=0),
    )(info, *attn, *one, *other)


def add(*terms):
    total = terms[0].astype(jnp.float32)
    for term in terms[1:]:
        total = total + term.astype(jnp.float32)
    return total.astype(jnp.bfloat16)


def local(queries, key_states, values, out_weight, pair_table, block_order):
    rank = lax.axis_index("ctx")
    head = lax.axis_index("head")
    y, low = head // 2, head % 2
    core, x = rank % 2, rank // 2 % 4

    def over_z(arr, i):
        return exchange(arr, masks[i] >> 3, 3, 2)

    columns = gather_z(out_weight)
    stacked = jnp.stack((key_states, values))
    masks = [pair_table[i, 0] for i in range(ROUNDS)]
    near = [exchange(stacked, mask & 7, 0, 3) for mask in masks]
    kv1 = over_z(near[0], 0)
    columns, near, kv1 = lax.optimization_barrier((columns, near, kv1))

    def block(step):
        return lax.dynamic_index_in_dim(columns, (y + step) % 4, 0, keepdims=False)

    mine = [block(0), to_y(block(3), -1), to_y(block(2), 2), to_y(block(1), 1)]
    kv2 = over_z(near[1], 1)
    mine, near, kv2 = lax.optimization_barrier((mine, near, kv2))
    mine = jnp.stack(mine)
    right = to_x(mine, -1)
    left = to_x(mine, 1)
    kv3 = over_z(near[2], 2)

    blk_dev = queries.shape[0] // BLOCK

    def ids(r):
        return lax.dynamic_slice_in_dim(block_order, r * blk_dev, blk_dev, 0)

    query_ids = ids(rank)
    key_ids = jnp.concatenate([query_ids] + [ids(jnp.bitwise_xor(rank, mask)) for mask in masks])
    attn = attend(query_ids, key_ids, queries, [stacked, kv1, kv2, kv3])

    above, below = to_y(attn, -1), to_y(attn, 1)
    right, left, attn = lax.optimization_barrier((right, left, attn))
    half = out_weight.shape[0] // 2
    upper = to_x(right[:, :half], -1)
    lower = to_x(left[:, half:], 1)
    cols = attn.shape[1] // 2
    far_y = [to_y(below[:, :cols], 1), to_y(above[:, cols:], -1)]
    gathered = [attn, above, jnp.concatenate(far_y, axis=1), below]

    def with_sibling(arr):
        return arr, from_sibling(arr)

    own, right, left = with_sibling(mine), with_sibling(right), with_sibling(left)
    sent_b, kept_b = project(core, (x + 1) % 4 // 2 != low, gathered, right, left)
    got_b = swap_low(sent_b)
    across = with_sibling(jnp.concatenate([upper, lower], axis=1))
    sent_a, kept_a = project(core, x // 2 != low, gathered, own, across)
    got_a = swap_low(sent_a)
    even, odd = add(kept_a, got_a), add(kept_b, got_b)
    at_left = x % 2 == 0
    return jnp.concatenate([jnp.where(at_left, even, odd), jnp.where(at_left, odd, even)], axis=1)


def solution(mesh):
    in_specs = (P("ctx", "head"), P("ctx", "head"), P("ctx", "head"), P("head", "ctx"), P(), P())
    return jax.shard_map(local, mesh=mesh, in_specs=in_specs, out_specs=P("ctx", "head"), check_vma=False)
```

```python
import math

import jax
import jax.numpy as jnp
from jax import lax
from jax.experimental import pallas as pl
from jax.experimental.pallas import tpu as pltpu
from jax.sharding import PartitionSpec as P

HD = 128
BLOCK = 128
ROUNDS = 3
SPAN = 4
GROUP = 2

CTX = [(z, x, c) for z in range(4) for x in range(4) for c in range(2)]
HEAD = [(y, s) for y in range(4) for s in range(2)]


def ctx_pairs(place):
    pairs = []
    for here in CTX:
        z, x, c = place(*here)
        pairs.append((here[0] * 8 + here[1] * 2 + here[2], z % 4 * 8 + x % 4 * 2 + c))
    return pairs


def head_pairs(place):
    pairs = []
    for here in HEAD:
        y, s = place(*here)
        pairs.append((here[0] * 2 + here[1], y % 4 * 2 + s))
    return pairs


def gather_z(arr):
    groups = [[z * 8 + x * 2 + c for z in range(4)] for x in range(4) for c in range(2)]
    return lax.all_gather(arr, "ctx", axis_index_groups=groups, axis=0)


def to_x(arr, step):
    return lax.ppermute(arr, "ctx", ctx_pairs(lambda z, x, c: (z, x + step, c)))


def from_sibling(arr):
    return lax.ppermute(arr, "ctx", ctx_pairs(lambda z, x, c: (z, x, 1 - c)))


def to_y(arr, step):
    return lax.ppermute(arr, "head", head_pairs(lambda y, s: (y + step, s)))


def swap_low(arr):
    return lax.ppermute(arr, "head", head_pairs(lambda y, s: (y, 1 - s)))


def exchange(arr, mask, shift, bits):
    def branch(m):
        return lambda held: lax.ppermute(held, "ctx", [(i, i ^ (m << shift)) for i in range(len(CTX))])

    return lax.switch(mask, [lambda held: held] + [branch(m) for m in range(1, 1 << bits)], arr)


def attend_kernel(qid, kid, q_ref, kv0, kv1, kv2, kv3, out, kc, vc, qs, ms, ls, acc):
    srcs = (kv0, kv1, kv2, kv3)
    hq = q_ref.shape[1] // HD
    blocks = q_ref.shape[0] // BLOCK
    factor = HD ** -0.5 * math.log2(math.e)
    width = SPAN * BLOCK
    tall = GROUP * BLOCK
    vc[...] = jnp.zeros_like(vc)

    def one_block(i, carry):
        me = qid[i]
        rows = pl.ds(pl.multiple_of(i * BLOCK, BLOCK), BLOCK)
        kc[0:BLOCK, :] = kv0[0, rows, :]
        vc[0:BLOCK, :] = kv0[1, rows, :]
        n = jnp.int32(1)
        for j in range(blocks * (ROUNDS + 1)):
            take = kid[j] < me
            src = srcs[j // blocks]
            lo = j % blocks * BLOCK

            @pl.when(take)
            def _():
                dst = pl.ds(pl.multiple_of(n * BLOCK, BLOCK), BLOCK)
                kc[dst, :] = src[0, lo:lo + BLOCK, :]
                vc[dst, :] = src[1, lo:lo + BLOCK, :]

            n = n + take.astype(jnp.int32)
        for h in range(hq):
            qs[h * BLOCK:(h + 1) * BLOCK, :] = q_ref[rows, h * HD:(h + 1) * HD]

        def step(t, first):
            base = pl.multiple_of(t * width, width)
            kk = kc[pl.ds(base, width), :]
            vv = vc[pl.ds(base, width), :]
            col = lax.broadcasted_iota(jnp.int32, (tall, width), 1)
            if first:
                row = lax.broadcasted_iota(jnp.int32, (tall, width), 0) & (BLOCK - 1)
                ok = (col <= row) | ((col >= BLOCK) & (col < n * BLOCK))
            else:
                ok = col < n * BLOCK - base
            for g in range(hq // GROUP):
                r = slice(g * tall, (g + 1) * tall)
                s = lax.dot_general(qs[r, :], kk, (((1,), (1,)), ((), ())), preferred_element_type=jnp.float32)
                s = jnp.where(ok, s, -jnp.inf)
                top = jnp.max(s, axis=1, keepdims=True)
                if not first:
                    before = ms[r, 0:1]
                    top = jnp.maximum(before, top)
                    keep = jnp.exp2((before - top) * factor)
                p = jnp.exp2((s - top) * factor)
                total = jnp.sum(p, axis=1, keepdims=True)
                o = jnp.dot(p.astype(jnp.bfloat16), vv, preferred_element_type=jnp.float32)
                if not first:
                    total = keep * ls[r, 0:1] + total
                    o = keep * acc[r, :] + o
                ms[r, :] = jnp.broadcast_to(top, (tall, HD))
                ls[r, :] = jnp.broadcast_to(total, (tall, HD))
                acc[r, :] = o

        step(0, True)

        def body(t, c):
            step(t, False)
            return c

        lax.fori_loop(1, lax.div(n + (SPAN - 1), jnp.int32(SPAN)), body, 0)
        for h in range(hq):
            r = slice(h * BLOCK, (h + 1) * BLOCK)
            out[rows, h * HD:(h + 1) * HD] = (acc[r, :] / ls[r, :]).astype(jnp.bfloat16)
        return carry

    lax.fori_loop(0, blocks, one_block, 0)


def attend(query_ids, key_ids, queries, kv_list):
    rows, cols = queries.shape
    tall = cols // HD * BLOCK
    room = rows * (ROUNDS + 1) + SPAN * BLOCK
    smem = pl.BlockSpec(memory_space=pltpu.SMEM)
    vmem = pl.BlockSpec(memory_space=pltpu.VMEM)
    return pl.pallas_call(
        attend_kernel,
        out_shape=jax.ShapeDtypeStruct(queries.shape, queries.dtype),
        in_specs=[smem, smem] + [vmem] * 5,
        out_specs=vmem,
        scratch_shapes=[pltpu.VMEM((room, HD), jnp.bfloat16)] * 2
        + [pltpu.VMEM((tall, HD), jnp.bfloat16)]
        + [pltpu.VMEM((tall, HD), jnp.float32)] * 3,
        compiler_params=pltpu.CompilerParams(vmem_limit_bytes=24 << 20),
        cost_estimate=pl.CostEstimate(flops=2 * rows * rows * 4 * cols * 2, bytes_accessed=4 << 20, transcendentals=rows * rows * 32),
    )(query_ids, key_ids, queries, *kv_list)


def project_kernel(info, a0, a1, a2, a3, *refs):
    one, other, sent, kept = refs[0:2], refs[2:4], refs[-2], refs[-1]
    core, one_sent = info[0], info[1]
    near_at = pl.ds(pl.multiple_of(core * 256, 256), 256)
    far_at = pl.ds(pl.multiple_of((1 - core) * 256, 256), 256)

    def product(weights, out):
        for w, at in zip(weights, (near_at, far_at)):
            total = None
            for step, a in enumerate((a0, a1, a2, a3)):
                term = jnp.dot(a[...], w[step], preferred_element_type=jnp.float32)
                total = term if total is None else total + term
            out[:, at] = total.astype(jnp.bfloat16)

    first = one_sent == 1

    @pl.when(first)
    def _():
        product(one, sent)
        product(other, kept)

    @pl.when(jnp.logical_not(first))
    def _():
        product(other, sent)
        product(one, kept)


def project(core, one_sent, attn, one, other):
    rows, depth = attn[0].shape
    cols = one[0].shape[2]
    smem = pl.BlockSpec(memory_space=pltpu.SMEM)
    vmem = pl.BlockSpec(memory_space=pltpu.VMEM)
    info = jnp.stack([core, one_sent.astype(jnp.int32)])
    return pl.pallas_call(
        project_kernel,
        out_shape=(jax.ShapeDtypeStruct((rows, 2 * cols), jnp.bfloat16),) * 2,
        in_specs=[smem] + [vmem] * 8,
        out_specs=(vmem,) * 2,
        compiler_params=pltpu.CompilerParams(vmem_limit_bytes=24 << 20),
        cost_estimate=pl.CostEstimate(flops=2 * rows * depth * 4 * cols * 4, bytes_accessed=13 << 20, transcendentals=0),
    )(info, *attn, *one, *other)


def add(*terms):
    total = terms[0].astype(jnp.float32)
    for term in terms[1:]:
        total = total + term.astype(jnp.float32)
    return total.astype(jnp.bfloat16)


def local(queries, key_states, values, out_weight, pair_table, block_order):
    rank = lax.axis_index("ctx")
    head = lax.axis_index("head")
    y, low = head // 2, head % 2
    core, x = rank % 2, rank // 2 % 4

    def over_z(arr, i):
        return exchange(arr, masks[i] >> 3, 3, 2)

    columns = gather_z(out_weight)
    stacked = jnp.stack((key_states, values))
    masks = [pair_table[i, 0] for i in range(ROUNDS)]
    near = [exchange(stacked, mask & 7, 0, 3) for mask in masks]
    columns, near = lax.optimization_barrier((columns, near))

    def block(step):
        return lax.dynamic_index_in_dim(columns, (y + step) % 4, 0, keepdims=False)

    mine = [block(0), to_y(block(3), -1), to_y(block(2), 2), to_y(block(1), 1)]
    kv1, kv2 = over_z(near[0], 0), over_z(near[1], 1)
    mine, near, kv1, kv2 = lax.optimization_barrier((mine, near, kv1, kv2))
    mine = jnp.stack(mine)
    right = to_x(mine, -1)
    left = to_x(mine, 1)
    kv3 = over_z(near[2], 2)

    blk_dev = queries.shape[0] // BLOCK

    def ids(r):
        return lax.dynamic_slice_in_dim(block_order, r * blk_dev, blk_dev, 0)

    query_ids = ids(rank)
    key_ids = jnp.concatenate([query_ids] + [ids(jnp.bitwise_xor(rank, mask)) for mask in masks])
    attn = attend(query_ids, key_ids, queries, [stacked, kv1, kv2, kv3])

    above, below = to_y(attn, -1), to_y(attn, 1)
    right, left, above, below = lax.optimization_barrier((right, left, above, below))
    half, cols = out_weight.shape[0] // 2, attn.shape[1] // 2
    parts = (below[:, :cols], above[:, cols:], right[:, :half], left[:, half:])
    parts = lax.optimization_barrier(parts)
    far_y = [to_y(parts[0], 1), to_y(parts[1], -1)]
    upper, lower = to_x(parts[2], -1), to_x(parts[3], 1)
    far_y, upper, lower = lax.optimization_barrier((far_y, upper, lower))
    gathered = [attn, above, jnp.concatenate(far_y, axis=1), below]

    def with_sibling(arr):
        return arr, from_sibling(arr)

    own, right, left = with_sibling(mine), with_sibling(right), with_sibling(left)
    sent_b, kept_b = project(core, (x + 1) % 4 // 2 != low, gathered, right, left)
    got_b = swap_low(sent_b)
    across = with_sibling(jnp.concatenate([upper, lower], axis=1))
    sent_a, kept_a = project(core, x // 2 != low, gathered, own, across)
    got_a = swap_low(sent_a)
    even, odd = add(kept_a, got_a), add(kept_b, got_b)
    at_left = x % 2 == 0
    return jnp.concatenate([jnp.where(at_left, even, odd), jnp.where(at_left, odd, even)], axis=1)


def solution(mesh):
    in_specs = (P("ctx", "head"), P("ctx", "head"), P("ctx", "head"), P("head", "ctx"), P(), P())
    return jax.shard_map(local, mesh=mesh, in_specs=in_specs, out_specs=P("ctx", "head"), check_vma=False)
```

```python
import math

import jax
import jax.numpy as jnp
from jax import lax
from jax.experimental import pallas as pl
from jax.experimental.pallas import tpu as pltpu
from jax.sharding import PartitionSpec as P

HD = 128
BLOCK = 128
ROUNDS = 3
SPAN = 4
GROUP = 2

CTX = [(z, x, c) for z in range(4) for x in range(4) for c in range(2)]
HEAD = [(y, s) for y in range(4) for s in range(2)]


def ctx_pairs(place):
    pairs = []
    for here in CTX:
        z, x, c = place(*here)
        pairs.append((here[0] * 8 + here[1] * 2 + here[2], z % 4 * 8 + x % 4 * 2 + c))
    return pairs


def head_pairs(place):
    pairs = []
    for here in HEAD:
        y, s = place(*here)
        pairs.append((here[0] * 2 + here[1], y % 4 * 2 + s))
    return pairs


def transpose_yz(arr):
    pairs = []
    for y, s in HEAD:
        for z, x, c in CTX:
            here = (y * 2 + s) * 32 + z * 8 + x * 2 + c
            pairs.append((here, (z * 2 + s) * 32 + y * 8 + x * 2 + c))
    return lax.ppermute(arr, ("head", "ctx"), pairs)


def to_y(arr, step):
    return lax.ppermute(arr, "head", head_pairs(lambda y, s: (y + step, s)))


def swap_low(arr):
    return lax.ppermute(arr, "head", head_pairs(lambda y, s: (y, 1 - s)))


def exchange(arr, mask, shift, bits):
    def branch(m):
        return lambda held: lax.ppermute(held, "ctx", [(i, i ^ (m << shift)) for i in range(len(CTX))])

    return lax.switch(mask, [lambda held: held] + [branch(m) for m in range(1, 1 << bits)], arr)


def attend_kernel(qid, kid, q_ref, kv0, kv1, kv2, kv3, out, kc, vc, qs, ms, ls, acc):
    srcs = (kv0, kv1, kv2, kv3)
    hq = q_ref.shape[1] // HD
    blocks = q_ref.shape[0] // BLOCK
    factor = HD ** -0.5 * math.log2(math.e)
    width = SPAN * BLOCK
    tall = GROUP * BLOCK
    vc[...] = jnp.zeros_like(vc)

    def one_block(i, carry):
        me = qid[i]
        rows = pl.ds(pl.multiple_of(i * BLOCK, BLOCK), BLOCK)
        kc[0:BLOCK, :] = kv0[0, rows, :]
        vc[0:BLOCK, :] = kv0[1, rows, :]
        n = jnp.int32(1)
        for j in range(blocks * (ROUNDS + 1)):
            take = kid[j] < me
            src = srcs[j // blocks]
            lo = j % blocks * BLOCK

            @pl.when(take)
            def _():
                dst = pl.ds(pl.multiple_of(n * BLOCK, BLOCK), BLOCK)
                kc[dst, :] = src[0, lo:lo + BLOCK, :]
                vc[dst, :] = src[1, lo:lo + BLOCK, :]

            n = n + take.astype(jnp.int32)
        for h in range(hq):
            qs[h * BLOCK:(h + 1) * BLOCK, :] = q_ref[rows, h * HD:(h + 1) * HD]

        def step(t, first):
            base = pl.multiple_of(t * width, width)
            kk = kc[pl.ds(base, width), :]
            vv = vc[pl.ds(base, width), :]
            col = lax.broadcasted_iota(jnp.int32, (tall, width), 1)
            if first:
                row = lax.broadcasted_iota(jnp.int32, (tall, width), 0) & (BLOCK - 1)
                ok = (col <= row) | ((col >= BLOCK) & (col < n * BLOCK))
            else:
                ok = col < n * BLOCK - base
            for g in range(hq // GROUP):
                r = slice(g * tall, (g + 1) * tall)
                s = lax.dot_general(qs[r, :], kk, (((1,), (1,)), ((), ())), preferred_element_type=jnp.float32)
                s = jnp.where(ok, s, -jnp.inf)
                top = jnp.max(s, axis=1, keepdims=True)
                if not first:
                    before = ms[r, 0:1]
                    top = jnp.maximum(before, top)
                    keep = jnp.exp2((before - top) * factor)
                p = jnp.exp2((s - top) * factor)
                total = jnp.sum(p, axis=1, keepdims=True)
                o = jnp.dot(p.astype(jnp.bfloat16), vv, preferred_element_type=jnp.float32)
                if not first:
                    total = keep * ls[r, 0:1] + total
                    o = keep * acc[r, :] + o
                ms[r, :] = jnp.broadcast_to(top, (tall, HD))
                ls[r, :] = jnp.broadcast_to(total, (tall, HD))
                acc[r, :] = o

        step(0, True)

        def body(t, c):
            step(t, False)
            return c

        lax.fori_loop(1, lax.div(n + (SPAN - 1), jnp.int32(SPAN)), body, 0)
        for h in range(hq):
            r = slice(h * BLOCK, (h + 1) * BLOCK)
            out[rows, h * HD:(h + 1) * HD] = (acc[r, :] / ls[r, :]).astype(jnp.bfloat16)
        return carry

    lax.fori_loop(0, blocks, one_block, 0)


def attend(query_ids, key_ids, queries, kv_list):
    rows, cols = queries.shape
    tall = cols // HD * BLOCK
    room = rows * (ROUNDS + 1) + SPAN * BLOCK
    smem = pl.BlockSpec(memory_space=pltpu.SMEM)
    vmem = pl.BlockSpec(memory_space=pltpu.VMEM)
    return pl.pallas_call(
        attend_kernel,
        out_shape=jax.ShapeDtypeStruct(queries.shape, queries.dtype),
        in_specs=[smem, smem] + [vmem] * 5,
        out_specs=vmem,
        scratch_shapes=[pltpu.VMEM((room, HD), jnp.bfloat16)] * 2
        + [pltpu.VMEM((tall, HD), jnp.bfloat16)]
        + [pltpu.VMEM((tall, HD), jnp.float32)] * 3,
        compiler_params=pltpu.CompilerParams(vmem_limit_bytes=24 << 20),
        cost_estimate=pl.CostEstimate(flops=2 * rows * rows * 4 * cols * 2, bytes_accessed=4 << 20, transcendentals=rows * rows * 32),
    )(query_ids, key_ids, queries, *kv_list)


def project_kernel(info, a0, a1, a2, a3, w, out):
    total = None
    for step, a in enumerate((a0, a1, a2, a3)):
        term = jnp.dot(a[...], w[info[1 + step], 0], preferred_element_type=jnp.float32)
        total = term if total is None else total + term
    out[...] = total.astype(jnp.bfloat16)


def project(info, attn, weight, start, count):
    rows, depth = attn[0].shape
    cols = weight.shape[3]
    whole = pl.BlockSpec(memory_space=pltpu.VMEM)
    return pl.pallas_call(
        project_kernel,
        out_shape=jax.ShapeDtypeStruct((rows, count * cols), jnp.bfloat16),
        grid_spec=pltpu.PrefetchScalarGridSpec(
            num_scalar_prefetch=1,
            grid=(count,),
            in_specs=[whole] * 4 + [pl.BlockSpec((4, 1, depth, cols), lambda j, info: (0, info[start] + j, 0, 0))],
            out_specs=pl.BlockSpec((rows, cols), lambda j, info: (0, j)),
        ),
        compiler_params=pltpu.CompilerParams(vmem_limit_bytes=48 << 20),
        cost_estimate=pl.CostEstimate(flops=2 * rows * depth * 4 * cols * count, bytes_accessed=12 << 20, transcendentals=0),
    )(info, *attn, weight)


def add(*terms):
    total = terms[0].astype(jnp.float32)
    for term in terms[1:]:
        total = total + term.astype(jnp.float32)
    return total.astype(jnp.bfloat16)


def gather_y(attn):
    half = attn.shape[1] // 2
    below = to_y(attn, 1)
    above = to_y(attn, -1)
    left = to_y(below[:, :half], 1)
    right = to_y(above[:, half:], -1)
    return [attn, above, jnp.concatenate([left, right], axis=1), below]


def local(queries, key_states, values, out_weight, pair_table, block_order):
    rank = lax.axis_index("ctx")
    head = lax.axis_index("head")
    y, low = head // 2, head % 2

    moved = transpose_yz(out_weight)
    stacked = jnp.stack((key_states, values))
    masks = [pair_table[i, 0] for i in range(ROUNDS)]
    near = [exchange(stacked, mask & 7, 0, 3) for mask in masks]
    moved, near = lax.optimization_barrier((moved, near))
    weight = lax.all_gather(moved, "ctx", axis=0)
    weight = weight.reshape((4, 8) + out_weight.shape)
    kv_list = [stacked] + [exchange(arr, mask >> 3, 3, 2) for arr, mask in zip(near, masks)]

    blk_dev = queries.shape[0] // BLOCK

    def ids(r):
        return lax.dynamic_slice_in_dim(block_order, r * blk_dev, blk_dev, 0)

    query_ids = ids(rank)
    key_ids = jnp.concatenate([query_ids] + [ids(jnp.bitwise_xor(rank, masks[i])) for i in range(ROUNDS)])
    attn = gather_y(attend(query_ids, key_ids, queries, kv_list))

    steps = jnp.arange(4, dtype=jnp.int32)
    sent, kept = 4 * (1 - low), 4 * low
    starts = jnp.stack([sent, sent + 1, sent + 2, kept])
    info = jnp.concatenate([jnp.zeros((1,), jnp.int32), (y + steps) % 4, starts]).astype(jnp.int32)
    arrived = [swap_low(project(info, attn, weight, 5 + i, n)) for i, n in enumerate((1, 1, 2))]
    ours = project(info, attn, weight, 8, 4)
    return add(ours, jnp.concatenate(arrived, axis=1))


def solution(mesh):
    in_specs = (P("ctx", "head"), P("ctx", "head"), P("ctx", "head"), P("head", "ctx"), P(), P())
    return jax.shard_map(local, mesh=mesh, in_specs=in_specs, out_specs=P("ctx", "head"), check_vma=False)
```

```python
import math

import jax
import jax.numpy as jnp
from jax import lax
from jax.experimental import pallas as pl
from jax.experimental.pallas import tpu as pltpu
from jax.sharding import PartitionSpec as P

HD = 128
BLOCK = 128
ROUNDS = 3
SPAN = 4
GROUP = 2

CTX = [(z, x, c) for z in range(4) for x in range(4) for c in range(2)]
HEAD = [(y, s) for y in range(4) for s in range(2)]


def ctx_pairs(place):
    pairs = []
    for here in CTX:
        z, x, c = place(*here)
        pairs.append((here[0] * 8 + here[1] * 2 + here[2], z % 4 * 8 + x % 4 * 2 + c))
    return pairs


def head_pairs(place):
    pairs = []
    for here in HEAD:
        y, s = place(*here)
        pairs.append((here[0] * 2 + here[1], y % 4 * 2 + s))
    return pairs


def transpose_yz(arr):
    pairs = []
    for y, s in HEAD:
        for z, x, c in CTX:
            here = (y * 2 + s) * 32 + z * 8 + x * 2 + c
            pairs.append((here, (z * 2 + s) * 32 + y * 8 + x * 2 + c))
    return lax.ppermute(arr, ("head", "ctx"), pairs)


def to_y(arr, step):
    return lax.ppermute(arr, "head", head_pairs(lambda y, s: (y + step, s)))


def swap_low(arr):
    return lax.ppermute(arr, "head", head_pairs(lambda y, s: (y, 1 - s)))


def exchange(arr, mask, shift, bits):
    def branch(m):
        return lambda held: lax.ppermute(held, "ctx", [(i, i ^ (m << shift)) for i in range(len(CTX))])

    return lax.switch(mask, [lambda held: held] + [branch(m) for m in range(1, 1 << bits)], arr)


def attend_kernel(qid, kid, q_ref, kv0, kv1, kv2, kv3, out, kc, vc, qs, ms, acc):
    srcs = (kv0, kv1, kv2, kv3)
    hq = q_ref.shape[1] // HD
    blocks = q_ref.shape[0] // BLOCK
    factor = HD ** -0.5 * math.log2(math.e)
    width = SPAN * BLOCK
    tall = GROUP * BLOCK
    vc[:, 0:HD] = jnp.zeros((vc.shape[0], HD), vc.dtype)
    vc[:, HD:] = jnp.ones((vc.shape[0], HD), vc.dtype)

    def one_block(i, carry):
        me = qid[i]
        rows = pl.ds(pl.multiple_of(i * BLOCK, BLOCK), BLOCK)
        kc[0:BLOCK, :] = kv0[0, rows, :]
        vc[0:BLOCK, 0:HD] = kv0[1, rows, :]
        n = jnp.int32(1)
        for j in range(blocks * (ROUNDS + 1)):
            take = kid[j] < me
            src = srcs[j // blocks]
            lo = j % blocks * BLOCK

            @pl.when(take)
            def _():
                dst = pl.ds(pl.multiple_of(n * BLOCK, BLOCK), BLOCK)
                kc[dst, :] = src[0, lo:lo + BLOCK, :]
                vc[dst, 0:HD] = src[1, lo:lo + BLOCK, :]

            n = n + take.astype(jnp.int32)
        for h in range(hq):
            qs[h * BLOCK:(h + 1) * BLOCK, :] = q_ref[rows, h * HD:(h + 1) * HD]

        def step(t, first):
            base = pl.multiple_of(t * width, width)
            kk = kc[pl.ds(base, width), :]
            vv = vc[pl.ds(base, width), :]
            col = lax.broadcasted_iota(jnp.int32, (tall, width), 1)
            if first:
                row = lax.broadcasted_iota(jnp.int32, (tall, width), 0) & (BLOCK - 1)
                ok = (col <= row) | ((col >= BLOCK) & (col < n * BLOCK))
            else:
                ok = col < n * BLOCK - base
            for g in range(hq // GROUP):
                r = slice(g * tall, (g + 1) * tall)
                s = lax.dot_general(qs[r, :], kk, (((1,), (1,)), ((), ())), preferred_element_type=jnp.float32)
                s = jnp.where(ok, s, -jnp.inf)
                top = jnp.max(s, axis=1, keepdims=True)
                if not first:
                    before = ms[r, 0:1]
                    top = jnp.maximum(before, top)
                    keep = jnp.exp2((before - top) * factor)
                p = jnp.exp2((s - top) * factor)
                o = jnp.dot(p.astype(jnp.bfloat16), vv, preferred_element_type=jnp.float32)
                if not first:
                    o = keep * acc[r, :] + o
                ms[r, :] = jnp.broadcast_to(top, (tall, HD))
                acc[r, :] = o

        step(0, True)

        def body(t, c):
            step(t, False)
            return c

        lax.fori_loop(1, lax.div(n + (SPAN - 1), jnp.int32(SPAN)), body, 0)
        for h in range(hq):
            r = slice(h * BLOCK, (h + 1) * BLOCK)
            out[rows, h * HD:(h + 1) * HD] = (acc[r, 0:HD] / acc[r, HD:]).astype(jnp.bfloat16)
        return carry

    lax.fori_loop(0, blocks, one_block, 0)


def attend(query_ids, key_ids, queries, kv_list):
    rows, cols = queries.shape
    tall = cols // HD * BLOCK
    room = rows * (ROUNDS + 1) + SPAN * BLOCK
    smem = pl.BlockSpec(memory_space=pltpu.SMEM)
    vmem = pl.BlockSpec(memory_space=pltpu.VMEM)
    return pl.pallas_call(
        attend_kernel,
        out_shape=jax.ShapeDtypeStruct(queries.shape, queries.dtype),
        in_specs=[smem, smem] + [vmem] * 5,
        out_specs=vmem,
        scratch_shapes=[
            pltpu.VMEM((room, HD), jnp.bfloat16),
            pltpu.VMEM((room, 2 * HD), jnp.bfloat16),
            pltpu.VMEM((tall, HD), jnp.bfloat16),
            pltpu.VMEM((tall, HD), jnp.float32),
            pltpu.VMEM((tall, 2 * HD), jnp.float32),
        ],
        compiler_params=pltpu.CompilerParams(vmem_limit_bytes=24 << 20),
        cost_estimate=pl.CostEstimate(flops=2 * rows * rows * 4 * cols * 2, bytes_accessed=4 << 20, transcendentals=rows * rows * 32),
    )(query_ids, key_ids, queries, *kv_list)


def project_kernel(info, a0, a1, a2, a3, w, out):
    total = None
    for step, a in enumerate((a0, a1, a2, a3)):
        term = jnp.dot(a[...], w[info[1 + step], 0], preferred_element_type=jnp.float32)
        total = term if total is None else total + term
    out[...] = total.astype(jnp.bfloat16)


def project(info, attn, weight, start, count):
    rows, depth = attn[0].shape
    cols = weight.shape[3]
    whole = pl.BlockSpec(memory_space=pltpu.VMEM)
    return pl.pallas_call(
        project_kernel,
        out_shape=jax.ShapeDtypeStruct((rows, count * cols), jnp.bfloat16),
        grid_spec=pltpu.PrefetchScalarGridSpec(
            num_scalar_prefetch=1,
            grid=(count,),
            in_specs=[whole] * 4 + [pl.BlockSpec((4, 1, depth, cols), lambda j, info: (0, info[start] + j, 0, 0))],
            out_specs=pl.BlockSpec((rows, cols), lambda j, info: (0, j)),
        ),
        compiler_params=pltpu.CompilerParams(vmem_limit_bytes=48 << 20),
        cost_estimate=pl.CostEstimate(flops=2 * rows * depth * 4 * cols * count, bytes_accessed=12 << 20, transcendentals=0),
    )(info, *attn, weight)


def add(*terms):
    total = terms[0].astype(jnp.float32)
    for term in terms[1:]:
        total = total + term.astype(jnp.float32)
    return total.astype(jnp.bfloat16)


def gather_y(attn):
    half = attn.shape[1] // 2
    below = to_y(attn, 1)
    above = to_y(attn, -1)
    left = to_y(below[:, :half], 1)
    right = to_y(above[:, half:], -1)
    return [attn, above, jnp.concatenate([left, right], axis=1), below]


def local(queries, key_states, values, out_weight, pair_table, block_order):
    rank = lax.axis_index("ctx")
    head = lax.axis_index("head")
    y, low = head // 2, head % 2

    moved = transpose_yz(out_weight)
    stacked = jnp.stack((key_states, values))
    masks = [pair_table[i, 0] for i in range(ROUNDS)]
    near = [exchange(stacked, mask & 7, 0, 3) for mask in masks]
    moved, near = lax.optimization_barrier((moved, near))
    weight = lax.all_gather(moved, "ctx", axis=0)
    weight = weight.reshape((4, 8) + out_weight.shape)
    kv_list = [stacked] + [exchange(arr, mask >> 3, 3, 2) for arr, mask in zip(near, masks)]

    blk_dev = queries.shape[0] // BLOCK

    def ids(r):
        return lax.dynamic_slice_in_dim(block_order, r * blk_dev, blk_dev, 0)

    query_ids = ids(rank)
    key_ids = jnp.concatenate([query_ids] + [ids(jnp.bitwise_xor(rank, masks[i])) for i in range(ROUNDS)])
    attn = gather_y(attend(query_ids, key_ids, queries, kv_list))

    steps = jnp.arange(4, dtype=jnp.int32)
    sent, kept = 4 * (1 - low), 4 * low
    starts = jnp.stack([sent, sent + 1, sent + 2, kept])
    info = jnp.concatenate([jnp.zeros((1,), jnp.int32), (y + steps) % 4, starts]).astype(jnp.int32)
    arrived = [swap_low(project(info, attn, weight, 5 + i, n)) for i, n in enumerate((1, 1, 2))]
    ours = project(info, attn, weight, 8, 4)
    return add(ours, jnp.concatenate(arrived, axis=1))


def solution(mesh):
    in_specs = (P("ctx", "head"), P("ctx", "head"), P("ctx", "head"), P("head", "ctx"), P(), P())
    return jax.shard_map(local, mesh=mesh, in_specs=in_specs, out_specs=P("ctx", "head"), check_vma=False)
```
